32 devices in a mesh: section: 2 (over x), ctx: 8 (over z, core), wshard: 2 (over y).
Axes of the slice: x: 2, y: 2, z: 4, core: 2. Of those that a mesh axis runs over, the one named last changes fastest.
Arguments:
- tokens: bfloat16 [2, 2, 1024, 768], P(None, 'wshard', 'ctx'), may hold values from -6 to 6
- block_order: int32 [2, 2, 8], P(None, 'wshard'), may hold values from 0 to 7, each once within a row
- cotangent: bfloat16 [2, 2, 1024, 768], P(None, 'wshard', 'ctx'), may hold values from -6 to 6
- attn_gain: bfloat16 [2, 768], P('section', ('ctx', 'wshard')), may hold values from 0.099609375 to 1.8984375
- qkv_weight: bfloat16 [2, 768, 2304], P('section', ('ctx', 'wshard')), may hold values from -0.21875 to 0.21875
- out_weight: bfloat16 [2, 768, 768], P('section', ('ctx', 'wshard')), may hold values from -5 to 5
- mlp_gain: bfloat16 [2, 768], P('section', ('ctx', 'wshard')), may hold values from 0.099609375 to 1.8984375
- in_weight: bfloat16 [2, 768, 2304], P('section', ('ctx', 'wshard')), may hold values from -0.21875 to 0.21875
- down_weight: bfloat16 [2, 1152, 768], P('section', ('ctx', 'wshard')), may hold values from -0.1875 to 0.1875
Outputs:
- activations: bfloat16 [2, 2, 2, 1024, 768], P('section', None, 'wshard', 'ctx')
- input_grads: float32 [2, 2, 2, 1024, 768], P('section', None, 'wshard', 'ctx')
- attn_gain_grad: float32 [2, 768], P('section', ('ctx', 'wshard'))
- qkv_grad: float32 [2, 768, 2304], P('section', ('ctx', 'wshard'))
- out_grad: float32 [2, 768, 768], P('section', ('ctx', 'wshard'))
- mlp_gain_grad: float32 [2, 768], P('section', ('ctx', 'wshard'))
- in_grad: float32 [2, 768, 2304], P('section', ('ctx', 'wshard'))
- down_grad: float32 [2, 1152, 768], P('section', ('ctx', 'wshard'))
The draws below stay inside these ranges and needn't reach their ends.
Inputs may be any that keep to these rules, and one draw needn't show every extreme that they name: Each block_order[m, w, :] is a permutation of the cycle devices: every block of 128 positions of a sequence sits on exactly one device.
All inputs are finite; a program needn't handle non-finite values.
Results may differ from the reference program's by a relative error of at most 0.03.
Values may be sent and summed in bfloat16 or wider, within the bound.
A program may use at most 256 MiB of HBM per device.

```python
import jax
import jax.numpy as jnp
from jax import lax

D = 768
HEADS = 12
HEAD_DIM = 64
FF = 1152
MICRO = 2
SEQ = 1024
N_SECTION = 2
N_CTX = 8
N_WSHARD = 2


def level_of(stream_key, extent, split, low, high):
    gain = 1.0
    for position, parts in split:
        draws = jax.random.uniform(jax.random.fold_in(jax.random.fold_in(stream_key, 6), position), (parts,), jnp.float32, low / len(split), high / len(split))
        gain = gain * jnp.repeat(jnp.exp(draws), extent[position] // parts).reshape((-1,) + (1,) * (len(extent) - 1 - position))
    return gain


def noise(rng, shape, deviation, bound, split=(), kind=jnp.bfloat16):
    result = deviation * jax.random.normal(rng, shape, jnp.float32)
    if split:
        result = result * level_of(rng, shape, split, -0.22, 0.18)
    return jnp.clip(result, -bound, bound).astype(kind)


def setup_inputs(seed: int = 0) -> dict:
    arg_keys = jax.random.split(jax.random.key(seed), 10)
    tokens = noise(arg_keys[0], (MICRO, N_WSHARD, SEQ, D), 1.0, 6.0, ((1, 2), (2, 8)))
    block_order = jax.vmap(lambda own: jax.random.permutation(own, N_CTX))(jax.random.split(arg_keys[1], MICRO * N_WSHARD)).reshape((MICRO, N_WSHARD, N_CTX)).astype(jnp.int32)
    cotangent = noise(arg_keys[2], (MICRO, N_WSHARD, SEQ, D), 1.0, 6.0, ((1, 2), (2, 8)))
    attn_gain = jnp.clip(1.0 + 0.18 * jax.random.normal(arg_keys[3], (N_SECTION, D), jnp.float32), 0.099609375, 1.8984375).astype(jnp.bfloat16)
    qkv_weight = noise(arg_keys[4], (N_SECTION, D, 3 * D), D ** -0.5, 0.21875, ((0, 2), (1, 16)))
    out_weight = noise(arg_keys[5], (N_SECTION, D, D), ((SEQ // D + 1) ** 0.5 * 0.6), 5.0, ((0, 2), (1, 16)))
    mlp_gain = jnp.clip(1.0 + 0.18 * jax.random.normal(arg_keys[6], (N_SECTION, D), jnp.float32), 0.099609375, 1.8984375).astype(jnp.bfloat16)
    in_weight = noise(arg_keys[7], (N_SECTION, D, 2 * FF), D ** -0.5, 0.21875, ((0, 2), (1, 16)))
    down_weight = noise(arg_keys[8], (N_SECTION, FF, D), FF ** -0.5, 0.1875, ((0, 2), (1, 16)))
    return {"tokens": tokens, "block_order": block_order, "cotangent": cotangent, "attn_gain": attn_gain, "qkv_weight": qkv_weight, "out_weight": out_weight, "mlp_gain": mlp_gain, "in_weight": in_weight, "down_weight": down_weight}


epsilon = 1e-05
rope_base = 160000.0
highest = lax.Precision.HIGHEST

@jax.custom_vjp
def low(v):
    return lax.optimization_barrier(v.astype(jnp.bfloat16)).astype(jnp.float32)

@jax.custom_vjp
def low_back(v):
    return v

def low_keep(v):
    return (low(v), None)

def low_pass(kept, grad):
    return (grad,)

def back_keep(v):
    return (v, None)

def back_low(kept, grad):
    return (low(grad),)
low.defvjp(low_keep, low_pass)
low_back.defvjp(back_keep, back_low)

def layer_norm(values):
    row_mean = lax.optimization_barrier(jnp.mean(values, axis=-1, keepdims=True))
    centered = values - row_mean
    variance = lax.optimization_barrier(jnp.mean(centered * centered, axis=-1, keepdims=True))
    return centered * lax.rsqrt(variance + epsilon)

def rotate(values, cosine, sine):
    half_width = values.shape[-1] // 2
    turned = jnp.concatenate([-values[..., half_width:], values[..., :half_width]], axis=-1)
    return values * cosine + turned * sine

def attend(query, key_all, value_all):
    seq_count, length, head_count, head_width = query.shape
    query_block = min(512, length)
    blocks = query.reshape(seq_count, length // query_block, query_block, head_count, head_width).transpose(1, 0, 2, 3, 4)

    def one_block(arrived):
        scores = low_back(jnp.einsum('bqhe,bkhe->bhqk', arrived, key_all, precision=highest) * head_width ** (-0.5))
        probs = jax.nn.softmax(scores, axis=-1)
        return jnp.einsum('bhqk,bkhe->bqhe', low(probs), value_all, precision=highest)
    results = lax.map(jax.checkpoint(one_block), blocks)
    return results.transpose(1, 0, 2, 3, 4).reshape(seq_count, length, head_count * head_width)

def block_layer(layer_in, cosine, sine, gain_one, w_qkv, w_out, gain_two, w_in, w_down):
    seq_count, length, _ = layer_in.shape
    normed = low(layer_norm(layer_in) * gain_one)
    mixed = low_back(jnp.einsum('bsd,df->bsf', normed, w_qkv, precision=highest))
    query = mixed[..., :D].reshape(seq_count, length, HEADS, HEAD_DIM)
    key_part = mixed[..., D:2 * D].reshape(seq_count, length, HEADS, HEAD_DIM)
    value = mixed[..., 2 * D:].reshape(seq_count, length, HEADS, HEAD_DIM)
    query = low(rotate(query, cosine, sine))
    key_part = low(rotate(key_part, cosine, sine))
    value = low(value)
    attended = low_back(attend(query, key_part, value))
    branch = low_back(jnp.einsum('bsd,de->bse', low(attended), w_out, precision=highest))
    hidden = layer_in + branch
    normed_two = low(layer_norm(hidden) * gain_two)
    gate_up = low_back(jnp.einsum('bsd,df->bsf', normed_two, w_in, precision=highest))
    product = low(jax.nn.gelu(gate_up[..., :FF], approximate=False) * gate_up[..., FF:])
    return hidden + low_back(jnp.einsum('bsf,fd->bsd', product, w_down, precision=highest))

def reference(tokens, block_order, cotangent, attn_gain, qkv_weight, out_weight, mlp_gain, in_weight, down_weight):
    seq_count = MICRO * N_WSHARD
    tok_rows = SEQ // N_CTX
    inputs = tokens.astype(jnp.float32).reshape(seq_count, SEQ, D)
    upstream = cotangent.astype(jnp.float32).reshape(seq_count, SEQ, D)
    positions = (block_order.astype(jnp.int32)[..., None] * tok_rows + jnp.arange(tok_rows, dtype=jnp.int32)).reshape(seq_count, SEQ)
    inverse = 1.0 / rope_base ** (jnp.arange(0, HEAD_DIM, 2, dtype=jnp.float32) / HEAD_DIM)
    angles = positions.astype(jnp.float32)[..., None] * inverse
    cosine = jnp.concatenate([jnp.cos(angles), jnp.cos(angles)], axis=-1)[:, :, None, :]
    sine = jnp.concatenate([jnp.sin(angles), jnp.sin(angles)], axis=-1)[:, :, None, :]

    def forward(layer_in, probe, gain_one, w_qkv, w_out, gain_two, w_in, w_down):
        first_out = block_layer(layer_in, cosine, sine, gain_one[0], w_qkv[0], w_out[0], gain_two[0], w_in[0], w_down[0])
        passed = low_back(low(first_out) + probe)
        second_out = block_layer(passed, cosine, sine, gain_one[1], w_qkv[1], w_out[1], gain_two[1], w_in[1], w_down[1])
        return (first_out, second_out)
    (first_out, second_out), pullback = jax.vjp(forward, inputs, jnp.zeros_like(inputs), attn_gain.astype(jnp.float32), qkv_weight.astype(jnp.float32), out_weight.astype(jnp.float32), mlp_gain.astype(jnp.float32), in_weight.astype(jnp.float32), down_weight.astype(jnp.float32))
    gradients = pullback((jnp.zeros_like(first_out), upstream))
    shape_out = (N_SECTION, MICRO, N_WSHARD, SEQ, D)
    section_outs = jnp.stack([first_out, second_out]).astype(jnp.bfloat16).reshape(shape_out)
    input_grads = jnp.stack([gradients[0], gradients[1]]).astype(jnp.float32).reshape(shape_out)
    return (section_outs, input_grads, gradients[2], gradients[3], gradients[4], gradients[5], gradients[6], gradients[7])
```

```python
import jax
import jax.numpy as jnp
from jax import lax
from jax.experimental import pallas as pl
from jax.experimental.pallas import tpu as pltpu
from jax.sharding import PartitionSpec as P

D = 768
HEADS = 12
HEAD_DIM = 64
FF = 1152


epsilon = 1e-05
rope_base = 160000.0


def shifted(x, axis, by):
    peers = lax.axis_size(axis)
    pairs = [(i, i + by) for i in range(peers) if 0 <= i + by < peers]
    return lax.ppermute(x, axis, pairs)


def normalize(values):
    row_mean = jnp.mean(values, axis=-1, keepdims=True)
    centered = values - row_mean
    variance = jnp.mean(centered * centered, axis=-1, keepdims=True)
    inverse = lax.rsqrt(variance + epsilon)
    return (centered * inverse, inverse)


def norm_back(grad_hat, normed, inverse):
    first_mean = jnp.mean(grad_hat, axis=-1, keepdims=True)
    second_mean = jnp.mean(grad_hat * normed, axis=-1, keepdims=True)
    return (grad_hat - first_mean - normed * second_mean) * inverse


def split_heads(values):
    return values.reshape(values.shape[0], HEADS, HEAD_DIM)


def join_heads(values):
    return values.reshape(values.shape[0], HEADS * HEAD_DIM)


def rotate_half(values):
    half_width = values.shape[-1] // 2
    return jnp.concatenate([-values[..., half_width:], values[..., :half_width]], axis=-1)


def rotate_back(values):
    half_width = values.shape[-1] // 2
    return jnp.concatenate([values[..., half_width:], -values[..., :half_width]], axis=-1)


def rotary(block_id, tok_rows):
    positions = (block_id * tok_rows + jnp.arange(tok_rows, dtype=jnp.int32)).astype(jnp.float32)
    inverse = 1.0 / rope_base ** (jnp.arange(0, HEAD_DIM, 2, dtype=jnp.float32) / HEAD_DIM)
    angles = positions[:, None] * inverse[None, :]
    cosine = jnp.concatenate([jnp.cos(angles), jnp.cos(angles)], axis=-1)[:, None, :]
    sine = jnp.concatenate([jnp.sin(angles), jnp.sin(angles)], axis=-1)[:, None, :]
    return (cosine, sine)


def absorb(state_now, arrived, query_heads):
    largest, running_sum, weighted = state_now
    key_rows, value_rows = arrived
    scores = jnp.einsum(
        "qhe,khe->hqk", query_heads, split_heads(key_rows), preferred_element_type=jnp.float32
    ) * HEAD_DIM ** (-0.5)
    new_max = jnp.maximum(largest, jnp.max(scores, axis=-1))
    shrink = jnp.exp(largest - new_max)
    exponents = jnp.exp(scores - new_max[:, :, None])
    running_sum = jnp.sum(exponents, axis=-1)
    weighted = weighted * shrink.T[:, :, None] + jnp.einsum(
        "hqk,khe->qhe",
        exponents.astype(jnp.bfloat16),
        split_heads(value_rows),
        preferred_element_type=jnp.float32,
    )
    return (new_max, running_sum, weighted)


def score_grads(query_heads, grad_heads, log_sums, deltas, key_heads, value_heads):
    scores = jnp.einsum(
        "qhe,khe->hqk", query_heads, key_heads, preferred_element_type=jnp.float32
    ) * HEAD_DIM ** (-0.5)
    weights = jnp.exp(scores - log_sums.T[:, :, None])
    upstream = jnp.einsum(
        "qhe,khe->hqk", grad_heads, value_heads, preferred_element_type=jnp.float32
    )
    grad_scores = (weights * (upstream - deltas.T[:, :, None])).astype(jnp.bfloat16)
    return (weights.astype(jnp.bfloat16), grad_scores)


def key_value_terms(query_heads, grad_heads, log_sums, deltas, key_heads, value_heads):
    weights_low, grad_scores = score_grads(
        query_heads, grad_heads, log_sums, deltas, key_heads, value_heads
    )
    key_part = jnp.einsum(
        "hqk,qhe->khe", grad_scores, query_heads, preferred_element_type=jnp.float32
    ) * HEAD_DIM ** (-0.5)
    value_part = jnp.einsum(
        "hqk,qhe->khe", weights_low, grad_heads, preferred_element_type=jnp.float32
    )
    return (key_part, value_part)


def forward_layer(layer_in, cosine, sine, params):
    gain_one, w_qkv, w_out, gain_two, w_in, w_down = params
    tok_rows = layer_in.shape[0]
    normed_one, _ = normalize(layer_in)
    mixed = jnp.dot(
        (normed_one * gain_one.astype(jnp.float32)).astype(jnp.bfloat16),
        w_qkv,
        preferred_element_type=jnp.float32,
    )
    query_raw = split_heads(mixed[:, :D])
    key_raw = split_heads(mixed[:, D : 2 * D])
    query_heads = (query_raw * cosine + rotate_half(query_raw) * sine).astype(jnp.bfloat16)
    key_rows = join_heads(key_raw * cosine + rotate_half(key_raw) * sine).astype(jnp.bfloat16)
    value_rows = mixed[:, 2 * D :].astype(jnp.bfloat16)
    start_state = (
        jnp.full((HEADS, tok_rows), -1e30, jnp.float32),
        jnp.zeros((HEADS, tok_rows), jnp.float32),
        jnp.zeros((tok_rows, HEADS, HEAD_DIM), jnp.float32),
    )
    both_rows = lax.all_gather(
        jnp.concatenate([key_rows, value_rows], axis=-1), "ctx", axis=0, tiled=True
    )
    key_rows, value_rows = both_rows[:, :D], both_rows[:, D:]
    final_state = absorb(start_state, (key_rows, value_rows), query_heads)
    largest, running_sum, weighted = final_state
    attended = join_heads(weighted / running_sum.T[:, :, None])
    log_sums = (largest + jnp.log(running_sum)).T
    hidden = layer_in + jnp.dot(
        attended.astype(jnp.bfloat16), w_out, preferred_element_type=jnp.float32
    )
    normed_two, _ = normalize(hidden)
    gate_up = jnp.dot(
        (normed_two * gain_two.astype(jnp.float32)).astype(jnp.bfloat16),
        w_in,
        preferred_element_type=jnp.float32,
    )
    product = (jax.nn.gelu(gate_up[:, :FF], approximate=False) * gate_up[:, FF:]).astype(
        jnp.bfloat16
    )
    layer_out = hidden + jnp.dot(product, w_down, preferred_element_type=jnp.float32)
    return (
        layer_out,
        (layer_in, hidden, gate_up, query_heads, key_rows, value_rows, attended, log_sums),
    )


def backward_layer(upstream, cosine, sine, params, saved, cycle_place):
    gain_one, w_qkv, w_out, gain_two, w_in, w_down = params
    layer_in, hidden, gate_up, query_heads, key_rows, value_rows, attended, log_sums = saved
    scale_factor = HEAD_DIM ** (-0.5)
    tok_rows = upstream.shape[0]
    grad_branch = upstream.astype(jnp.bfloat16)
    gate_part = gate_up[:, :FF]
    up_part = gate_up[:, FF:]
    activated, gelu_pull = jax.vjp(
        lambda gate_in: jax.nn.gelu(gate_in, approximate=False), gate_part
    )
    product = (activated * up_part).astype(jnp.bfloat16)
    grad_down = jnp.einsum("tf,td->fd", product, grad_branch, preferred_element_type=jnp.float32)
    grad_product = jnp.einsum("td,fd->tf", grad_branch, w_down, preferred_element_type=jnp.float32)
    grad_gate = gelu_pull(grad_product * up_part)[0]
    grad_gate_up = jnp.concatenate([grad_gate, grad_product * activated], axis=-1).astype(
        jnp.bfloat16
    )
    normed_two, inverse_two = normalize(hidden)
    gain_two_full = gain_two.astype(jnp.float32)
    grad_in = jnp.einsum(
        "td,tf->df",
        (normed_two * gain_two_full).astype(jnp.bfloat16),
        grad_gate_up,
        preferred_element_type=jnp.float32,
    )
    grad_normed_two = jnp.einsum(
        "tf,df->td", grad_gate_up, w_in, preferred_element_type=jnp.float32
    )
    grad_gain_two = jnp.sum(grad_normed_two * normed_two, axis=0)
    grad_hidden = upstream + norm_back(grad_normed_two * gain_two_full, normed_two, inverse_two)
    grad_attn_out = grad_hidden.astype(jnp.bfloat16)
    grad_out = jnp.einsum(
        "td,te->de",
        attended.astype(jnp.bfloat16),
        grad_attn_out,
        preferred_element_type=jnp.float32,
    )
    grad_attended = split_heads(
        jnp.einsum("te,de->td", grad_attn_out, w_out, preferred_element_type=jnp.float32).astype(
            jnp.bfloat16
        )
    )
    deltas = jnp.sum(grad_attended.astype(jnp.float32) * split_heads(attended), axis=-1)
    stats = jnp.concatenate([log_sums, deltas], axis=-1)
    stats_high = lax.reduce_precision(stats, 8, 7)
    packed = jnp.concatenate(
        [
            join_heads(query_heads),
            join_heads(grad_attended),
            stats_high.astype(jnp.bfloat16),
            (stats - stats_high).astype(jnp.bfloat16),
        ],
        axis=-1,
    )
    packed = lax.all_gather(packed, "ctx", axis=0, tiled=True)
    queries_all, grads_all = packed[:, :D], packed[:, D : 2 * D]
    stats_all = packed[:, 2 * D :].astype(jnp.float32)
    stats_all = stats_all[:, : 2 * HEADS] + stats_all[:, 2 * HEADS :]
    all_logs, all_deltas = stats_all[:, :HEADS], stats_all[:, HEADS:]
    empty_heads = jnp.zeros((tok_rows, HEADS, HEAD_DIM), jnp.float32)
    key_heads = split_heads(key_rows)
    value_heads = split_heads(value_rows)
    _, grad_scores = score_grads(
        query_heads, grad_attended, log_sums, deltas, key_heads, value_heads
    )
    grad_query = (
        jnp.einsum("hqk,khe->qhe", grad_scores, key_heads, preferred_element_type=jnp.float32)
        * scale_factor
    )
    own_start = cycle_place * tok_rows
    own_keys = split_heads(lax.dynamic_slice_in_dim(key_rows, own_start, tok_rows, 0))
    own_values = split_heads(lax.dynamic_slice_in_dim(value_rows, own_start, tok_rows, 0))
    total_rows = queries_all.shape[0]
    block_rows = min(1024, total_rows)
    block_count = total_rows // block_rows

    def query_block(running, pieces):
        block_queries, block_grads, block_logs, block_deltas = pieces
        key_part, value_part = key_value_terms(
            split_heads(block_queries),
            split_heads(block_grads),
            block_logs,
            block_deltas,
            own_keys,
            own_values,
        )
        return ((running[0] + key_part, running[1] + value_part), None)

    stacked = (
        queries_all.reshape(block_count, block_rows, D),
        grads_all.reshape(block_count, block_rows, D),
        all_logs.reshape(block_count, block_rows, HEADS),
        all_deltas.reshape(block_count, block_rows, HEADS),
    )
    if block_count == 1:
        grad_key, grad_value_heads = key_value_terms(
            split_heads(queries_all),
            split_heads(grads_all),
            all_logs,
            all_deltas,
            own_keys,
            own_values,
        )
    else:
        (grad_key, grad_value_heads), _ = lax.scan(query_block, (empty_heads, empty_heads), stacked)
    grad_value = join_heads(grad_value_heads)
    query_grad_raw = grad_query * cosine + rotate_back(grad_query * sine)
    key_grad_raw = grad_key * cosine + rotate_back(grad_key * sine)
    grad_mixed = jnp.concatenate(
        [join_heads(query_grad_raw), join_heads(key_grad_raw), grad_value], axis=-1
    ).astype(jnp.bfloat16)
    normed_one, inverse_one = normalize(layer_in)
    gain_one_full = gain_one.astype(jnp.float32)
    grad_qkv = jnp.einsum(
        "td,tf->df",
        (normed_one * gain_one_full).astype(jnp.bfloat16),
        grad_mixed,
        preferred_element_type=jnp.float32,
    )
    grad_normed_one = jnp.einsum("tf,df->td", grad_mixed, w_qkv, preferred_element_type=jnp.float32)
    grad_gain_one = jnp.sum(grad_normed_one * normed_one, axis=0)
    grad_layer_in = grad_hidden + norm_back(
        grad_normed_one * gain_one_full, normed_one, inverse_one
    )
    return (grad_layer_in, (grad_gain_one, grad_qkv, grad_out, grad_gain_two, grad_in, grad_down))


def keep_slot(buffer, batch_slot, value, is_valid):
    previous = lax.dynamic_index_in_dim(buffer, batch_slot, 0, keepdims=False)
    return lax.dynamic_update_index_in_dim(
        buffer, jnp.where(is_valid, value, previous), batch_slot, 0
    )

MESH = pl.DeviceIdType.MESH


def greet(chips):
    me = lax.axis_index("ctx")
    chip, core = me // 2, me % 2
    w = lax.axis_index("wshard")
    barrier = pltpu.get_barrier_semaphore()
    peers = [{"ctx": ((chip + d) % chips) * 2 + core} for d in range(1, chips)]
    peers += [{"wshard": 1 - w}, {"ctx": chip * 2 + 1 - core}]
    for peer in peers:
        pl.semaphore_signal(barrier, inc=1, device_id=peer, device_id_type=MESH)
    pl.semaphore_wait(barrier, len(peers))


def gather_kernel(chips, count, *refs):
    ins, outs = refs[:count], refs[count : 2 * count]
    own_sem, z_send, z_recv, y_send, y_recv, c_send, c_recv = refs[2 * count :]
    me = lax.axis_index("ctx")
    chip, core = me // 2, me % 2
    w = lax.axis_index("wshard")

    def slot(chip_at, core_at, w_at):
        return (chip_at * 2 + core_at) * 2 + w_at

    greet(chips)
    own = slot(chip, core, w)

    def to_chip(a, d):
        return pltpu.make_async_remote_copy(
            ins[a].at[0], outs[a].at[own], z_send.at[a, d - 1], z_recv.at[a, d - 1],
            device_id={"ctx": ((chip + d) % chips) * 2 + core}, device_id_type=MESH)

    def to_wide(a, d):
        at = slot((chip - d + chips) % chips, core, w)
        source = ins[a].at[0] if d == 0 else outs[a].at[at]
        return pltpu.make_async_remote_copy(
            source, outs[a].at[at], y_send.at[a, d], y_recv.at[a, d],
            device_id={"wshard": 1 - w}, device_id_type=MESH)

    def to_core(a, d, far):
        at = slot((chip - d + chips) % chips, core, 1 - w if far else w)
        source = ins[a].at[0] if d == 0 and not far else outs[a].at[at]
        index = d + chips * far
        return pltpu.make_async_remote_copy(
            source, outs[a].at[at], c_send.at[a, index], c_recv.at[a, index],
            device_id={"ctx": chip * 2 + 1 - core}, device_id_type=MESH)

    def keep(a):
        return pltpu.make_async_copy(ins[a].at[0], outs[a].at[own], own_sem.at[a])

    for a in range(count):
        to_wide(a, 0).start()
        for d in range(1, chips):
            to_chip(a, d).start()
        to_core(a, 0, 0).start()
        keep(a).start()
    for a in range(count):
        for d in range(1, chips):
            to_chip(a, d).wait_recv()
            to_wide(a, d).start()
            to_core(a, d, 0).start()
        for d in range(chips):
            to_wide(a, d).wait_recv()
            to_core(a, d, 1).start()
    for a in range(count):
        keep(a).wait()
        for d in range(chips):
            for far in range(2):
                to_core(a, d, far).wait_recv()
    for a in range(count):
        for d in range(1, chips):
            to_chip(a, d).wait_send()
        for d in range(chips):
            to_wide(a, d).wait_send()
            for far in range(2):
                to_core(a, d, far).wait_send()


def gather_shards(arrays, chips):
    count = len(arrays)
    shards = chips * 4
    return pl.pallas_call(
        lambda *refs: gather_kernel(chips, count, *refs),
        out_shape=[jax.ShapeDtypeStruct((shards,) + x.shape[1:], x.dtype) for x in arrays],
        in_specs=[pl.BlockSpec(memory_space=pl.ANY)] * count,
        out_specs=[pl.BlockSpec(memory_space=pl.ANY)] * count,
        scratch_shapes=[
            pltpu.SemaphoreType.DMA((count,)),
            pltpu.SemaphoreType.DMA((count, chips - 1)),
            pltpu.SemaphoreType.DMA((count, chips - 1)),
            pltpu.SemaphoreType.DMA((count, chips)),
            pltpu.SemaphoreType.DMA((count, chips)),
            pltpu.SemaphoreType.DMA((count, 2 * chips)),
            pltpu.SemaphoreType.DMA((count, 2 * chips)),
        ],
        compiler_params=pltpu.CompilerParams(collective_id=0, has_side_effects=True),
        name="gather_shards",
    )(*arrays)


def scatter_kernel(chips, count, *refs):
    ins, outs = refs[:count], refs[count : 2 * count]
    rest = refs[2 * count :]
    from_core, from_wide, from_chip = rest[:count], rest[count : 2 * count], rest[2 * count : 3 * count]
    half, near = rest[3 * count : 4 * count], rest[4 * count : 5 * count]
    c_send, c_recv, y_send, y_recv, z_send, z_recv = rest[5 * count :]
    me = lax.axis_index("ctx")
    chip, core = me // 2, me % 2
    w = lax.axis_index("wshard")

    def slot(chip_at, core_at, w_at):
        return (chip_at * 2 + core_at) * 2 + w_at

    def wide(value):
        return value.astype(jnp.float32)

    greet(chips)

    def to_core(a, d, far):
        at = slot((chip + d) % chips, 1 - core, 1 - w if far else w)
        return pltpu.make_async_remote_copy(
            ins[a].at[at], from_core[a].at[d, far], c_send.at[a, d, far], c_recv.at[a, d, far],
            device_id={"ctx": chip * 2 + 1 - core}, device_id_type=MESH)

    def to_wide(a, d):
        return pltpu.make_async_remote_copy(
            half[a].at[d], from_wide[a].at[d], y_send.at[a, d], y_recv.at[a, d],
            device_id={"wshard": 1 - w}, device_id_type=MESH)

    def to_chip(a, d):
        return pltpu.make_async_remote_copy(
            near[a].at[d - 1], from_chip[a].at[d - 1], z_send.at[a, d - 1], z_recv.at[a, d - 1],
            device_id={"ctx": ((chip + d) % chips) * 2 + core}, device_id_type=MESH)

    order = list(range(1, chips)) + [0]
    for far in (1, 0):
        for a in range(count):
            for d in order:
                to_core(a, d, far).start()
    for a in range(count):
        for d in order:
            to_core(a, d, 1).wait_recv()
            mine = ins[a][slot((chip + d) % chips, core, 1 - w)]
            half[a][d] = (wide(mine) + wide(from_core[a][d, 1])).astype(jnp.bfloat16)
            to_wide(a, d).start()
    for a in range(count):
        for d in order:
            to_core(a, d, 0).wait_recv()
            to_wide(a, d).wait_recv()
            mine = ins[a][slot((chip + d) % chips, core, w)]
            total = wide(mine) + wide(from_core[a][d, 0]) + wide(from_wide[a][d])
            if d == 0:
                outs[a][0] = total
            else:
                near[a][d - 1] = total.astype(jnp.bfloat16)
                to_chip(a, d).start()
    for a in range(count):
        total = outs[a][0]
        for d in range(1, chips):
            to_chip(a, d).wait_recv()
            total = total + wide(from_chip[a][d - 1])
        outs[a][0] = total
    for a in range(count):
        for d in range(chips):
            to_core(a, d, 0).wait_send()
            to_core(a, d, 1).wait_send()
            to_wide(a, d).wait_send()
            if d:
                to_chip(a, d).wait_send()


def scatter_sums(arrays, chips):
    count = len(arrays)
    tails = [x.shape[1:] for x in arrays]

    def slots(*lead):
        return [pltpu.VMEM(lead + tail, jnp.bfloat16) for tail in tails]

    return pl.pallas_call(
        lambda *refs: scatter_kernel(chips, count, *refs),
        out_shape=[jax.ShapeDtypeStruct((1,) + tail, jnp.float32) for tail in tails],
        in_specs=[pl.BlockSpec(memory_space=pltpu.VMEM)] * count,
        out_specs=[pl.BlockSpec(memory_space=pltpu.VMEM)] * count,
        scratch_shapes=slots(chips, 2) + slots(chips) + slots(chips - 1) + slots(chips) + slots(chips - 1)
        + [
            pltpu.SemaphoreType.DMA((count, chips, 2)),
            pltpu.SemaphoreType.DMA((count, chips, 2)),
            pltpu.SemaphoreType.DMA((count, chips)),
            pltpu.SemaphoreType.DMA((count, chips)),
            pltpu.SemaphoreType.DMA((count, chips - 1)),
            pltpu.SemaphoreType.DMA((count, chips - 1)),
        ],
        compiler_params=pltpu.CompilerParams(
            collective_id=1, has_side_effects=True, vmem_limit_bytes=48 * 1024 * 1024
        ),
        name="scatter_sums",
    )(*arrays)


def use_kernels():
    cycle, wides = lax.axis_size("ctx"), lax.axis_size("wshard")
    return wides == 2 and cycle % 2 == 0 and 4 <= cycle <= 8


def gather_params(attn_gain, qkv_weight, out_weight, mlp_gain, in_weight, down_weight):
    chips = lax.axis_size("ctx") // 2
    gain_width = attn_gain.shape[1]
    gains = jnp.concatenate([attn_gain, mlp_gain], axis=0)
    gains = jnp.pad(gains, ((0, 14), (0, 128 - gain_width)))[None]
    gains, qkv, out, into, down = gather_shards(
        (gains, qkv_weight, out_weight, in_weight, down_weight), chips
    )
    return (
        gains[:, 0, :gain_width].reshape(D),
        qkv.reshape(D, -1),
        out.reshape(D, -1),
        gains[:, 1, :gain_width].reshape(D),
        into.reshape(D, -1),
        down.reshape(-1, D),
    )


def scatter_grads(summed):
    shards = lax.axis_size("ctx") * 2
    gain_one, qkv, out, gain_two, into, down = summed
    gain_width = gain_one.shape[0] // shards
    gains = jnp.stack([gain_one.reshape(shards, gain_width), gain_two.reshape(shards, gain_width)], axis=1)
    gains = jnp.pad(gains, ((0, 0), (0, 14), (0, 128 - gain_width)))
    parts = [x.reshape(shards, x.shape[0] // shards, x.shape[1]) for x in (down, into, out, qkv)]
    parts = [x.astype(jnp.bfloat16) for x in [gains] + parts]
    gains, down, into, out, qkv = scatter_sums(parts, shards // 4)
    return (gains[:, 0, :gain_width], qkv, out, gains[:, 1, :gain_width], into, down)


def body(
    tokens,
    block_order,
    cotangent,
    attn_gain,
    qkv_weight,
    out_weight,
    mlp_gain,
    in_weight,
    down_weight,
):
    if use_kernels():
        params = gather_params(
            attn_gain, qkv_weight, out_weight, mlp_gain, in_weight, down_weight
        )
    else:
        gathered = (
            lax.all_gather(attn_gain, ("ctx", "wshard"), axis=1, tiled=True),
            lax.all_gather(qkv_weight, ("ctx", "wshard"), axis=1, tiled=True),
            lax.all_gather(out_weight, ("ctx", "wshard"), axis=1, tiled=True),
            lax.all_gather(mlp_gain, ("ctx", "wshard"), axis=1, tiled=True),
            lax.all_gather(in_weight, ("ctx", "wshard"), axis=1, tiled=True),
            lax.all_gather(down_weight, ("ctx", "wshard"), axis=1, tiled=True),
        )
        params = tuple((whole[0] for whole in gathered))
    section_id = lax.axis_index("section")
    section_count = lax.axis_size("section")
    cycle_place = lax.axis_index("ctx")
    micro_count = tokens.shape[0]
    tok_rows = tokens.shape[2]
    tick_count = micro_count + section_count - 1
    received = jnp.zeros((tok_rows, D), jnp.bfloat16)
    section_outs = jnp.zeros((micro_count, tok_rows, D), jnp.bfloat16)
    saved_all = None
    for tick in range(tick_count):
        batch_index = tick - section_id
        is_valid = (batch_index >= 0) & (batch_index < micro_count)
        batch_slot = jnp.clip(batch_index, 0, micro_count - 1)
        own_rows = tokens[batch_slot, 0]
        layer_in = jnp.where(section_id == 0, own_rows, received).astype(jnp.float32)
        cosine, sine = rotary(block_order[batch_slot, 0, cycle_place], tok_rows)
        layer_out, saved = forward_layer(layer_in, cosine, sine, params)
        if saved_all is None:
            saved_all = tuple(
                (jnp.zeros((micro_count,) + item.shape, item.dtype) for item in saved)
            )
        saved_all = tuple(
            (
                keep_slot(buffer, batch_slot, item, is_valid)
                for buffer, item in zip(saved_all, saved)
            )
        )
        outgoing = layer_out.astype(jnp.bfloat16)
        section_outs = keep_slot(section_outs, batch_slot, outgoing, is_valid)
        received = shifted(outgoing, "section", 1)
    grad_received = jnp.zeros((tok_rows, D), jnp.bfloat16)
    input_grads = jnp.zeros((micro_count, tok_rows, D), jnp.float32)
    summed = None
    for tick in range(tick_count):
        batch_index = tick - (section_count - 1 - section_id)
        is_valid = (batch_index >= 0) & (batch_index < micro_count)
        batch_slot = jnp.clip(batch_index, 0, micro_count - 1)
        upstream = jnp.where(
            section_id == section_count - 1, cotangent[batch_slot, 0], grad_received
        ).astype(jnp.float32)
        cosine, sine = rotary(block_order[batch_slot, 0, cycle_place], tok_rows)
        saved = tuple(
            (
                lax.dynamic_index_in_dim(buffer, batch_slot, 0, keepdims=False)
                for buffer in saved_all
            )
        )
        grad_layer_in, raw_grads = backward_layer(
            upstream, cosine, sine, params, saved, cycle_place
        )
        weight_grads = tuple(
            (jnp.where(is_valid, grad_term, jnp.zeros_like(grad_term)) for grad_term in raw_grads)
        )
        outgoing = grad_layer_in.astype(jnp.bfloat16)
        kept_grad = jnp.where(section_id == 0, grad_layer_in, outgoing.astype(jnp.float32))
        input_grads = keep_slot(input_grads, batch_slot, kept_grad, is_valid)
        summed = (
            weight_grads
            if summed is None
            else tuple((left + right for left, right in zip(summed, weight_grads)))
        )
        grad_received = shifted(outgoing, "section", -1)
    if use_kernels():
        summed = scatter_grads(summed)
    else:
        raised = [grad_term[None] for grad_term in summed]
        summed = (
            lax.psum_scatter(raised[0], ("ctx", "wshard"), scatter_dimension=1, tiled=True),
            lax.psum_scatter(raised[1], ("ctx", "wshard"), scatter_dimension=1, tiled=True),
            lax.psum_scatter(raised[2], ("ctx", "wshard"), scatter_dimension=1, tiled=True),
            lax.psum_scatter(raised[3], ("ctx", "wshard"), scatter_dimension=1, tiled=True),
            lax.psum_scatter(raised[4], ("ctx", "wshard"), scatter_dimension=1, tiled=True),
            lax.psum_scatter(raised[5], ("ctx", "wshard"), scatter_dimension=1, tiled=True),
        )
    return (
        section_outs[None, :, None],
        input_grads[None, :, None],
        summed[0],
        summed[1],
        summed[2],
        summed[3],
        summed[4],
        summed[5],
    )


def solution(mesh):
    in_specs = (
        P(None, "wshard", "ctx", None),
        P(None, "wshard", None),
        P(None, "wshard", "ctx", None),
        P("section", ("ctx", "wshard")),
        P("section", ("ctx", "wshard"), None),
        P("section", ("ctx", "wshard"), None),
        P("section", ("ctx", "wshard")),
        P("section", ("ctx", "wshard"), None),
        P("section", ("ctx", "wshard"), None),
    )
    out_specs = (
        P("section", None, "wshard", "ctx", None),
        P("section", None, "wshard", "ctx", None),
        P("section", ("ctx", "wshard")),
        P("section", ("ctx", "wshard"), None),
        P("section", ("ctx", "wshard"), None),
        P("section", ("ctx", "wshard")),
        P("section", ("ctx", "wshard"), None),
        P("section", ("ctx", "wshard"), None),
    )
    return jax.shard_map(body, mesh=mesh, in_specs=in_specs, out_specs=out_specs, check_vma=False)
```

```python
import jax
import jax.numpy as jnp
from jax import lax
from jax.experimental import pallas as pl
from jax.experimental.pallas import tpu as pltpu
from jax.sharding import PartitionSpec as P

D = 768
HEADS = 12
HEAD_DIM = 64
FF = 1152


epsilon = 1e-05
rope_base = 160000.0


def shifted(x, axis, by):
    peers = lax.axis_size(axis)
    pairs = [(i, i + by) for i in range(peers) if 0 <= i + by < peers]
    return lax.ppermute(x, axis, pairs)


def normalize(values):
    row_mean = jnp.mean(values, axis=-1, keepdims=True)
    centered = values - row_mean
    variance = jnp.mean(centered * centered, axis=-1, keepdims=True)
    inverse = lax.rsqrt(variance + epsilon)
    return (centered * inverse, inverse)


def norm_back(grad_hat, normed, inverse):
    first_mean = jnp.mean(grad_hat, axis=-1, keepdims=True)
    second_mean = jnp.mean(grad_hat * normed, axis=-1, keepdims=True)
    return (grad_hat - first_mean - normed * second_mean) * inverse


def split_heads(values):
    return values.reshape(values.shape[0], HEADS, HEAD_DIM)


def join_heads(values):
    return values.reshape(values.shape[0], HEADS * HEAD_DIM)


def rotate_half(values):
    half_width = values.shape[-1] // 2
    return jnp.concatenate([-values[..., half_width:], values[..., :half_width]], axis=-1)


def rotate_back(values):
    half_width = values.shape[-1] // 2
    return jnp.concatenate([values[..., half_width:], -values[..., :half_width]], axis=-1)


def rotary(block_id, tok_rows):
    positions = (block_id * tok_rows + jnp.arange(tok_rows, dtype=jnp.int32)).astype(jnp.float32)
    inverse = 1.0 / rope_base ** (jnp.arange(0, HEAD_DIM, 2, dtype=jnp.float32) / HEAD_DIM)
    angles = positions[:, None] * inverse[None, :]
    cosine = jnp.concatenate([jnp.cos(angles), jnp.cos(angles)], axis=-1)[:, None, :]
    sine = jnp.concatenate([jnp.sin(angles), jnp.sin(angles)], axis=-1)[:, None, :]
    return (cosine, sine)


def absorb(state_now, arrived, query_heads):
    largest, running_sum, weighted = state_now
    key_rows, value_rows = arrived
    scores = jnp.einsum(
        "qhe,khe->hqk", query_heads, split_heads(key_rows), preferred_element_type=jnp.float32
    ) * HEAD_DIM ** (-0.5)
    new_max = jnp.maximum(largest, jnp.max(scores, axis=-1))
    shrink = jnp.exp(largest - new_max)
    exponents = jnp.exp(scores - new_max[:, :, None])
    running_sum = jnp.sum(exponents, axis=-1)
    weighted = weighted * shrink.T[:, :, None] + jnp.einsum(
        "hqk,khe->qhe",
        exponents.astype(jnp.bfloat16),
        split_heads(value_rows),
        preferred_element_type=jnp.float32,
    )
    return (new_max, running_sum, weighted)


def score_grads(query_heads, grad_heads, log_sums, deltas, key_heads, value_heads):
    scores = jnp.einsum(
        "qhe,khe->hqk", query_heads, key_heads, preferred_element_type=jnp.float32
    ) * HEAD_DIM ** (-0.5)
    weights = jnp.exp(scores - log_sums.T[:, :, None])
    upstream = jnp.einsum(
        "qhe,khe->hqk", grad_heads, value_heads, preferred_element_type=jnp.float32
    )
    grad_scores = (weights * (upstream - deltas.T[:, :, None])).astype(jnp.bfloat16)
    return (weights.astype(jnp.bfloat16), grad_scores)


def key_value_terms(query_heads, grad_heads, log_sums, deltas, key_heads, value_heads):
    weights_low, grad_scores = score_grads(
        query_heads, grad_heads, log_sums, deltas, key_heads, value_heads
    )
    key_part = jnp.einsum(
        "hqk,qhe->khe", grad_scores, query_heads, preferred_element_type=jnp.float32
    ) * HEAD_DIM ** (-0.5)
    value_part = jnp.einsum(
        "hqk,qhe->khe", weights_low, grad_heads, preferred_element_type=jnp.float32
    )
    return (key_part, value_part)


def forward_layer(layer_in, cosine, sine, params):
    gain_one, w_qkv, w_out, gain_two, w_in, w_down = params
    tok_rows = layer_in.shape[0]
    normed_one, _ = normalize(layer_in)
    mixed = jnp.dot(
        (normed_one * gain_one.astype(jnp.float32)).astype(jnp.bfloat16),
        w_qkv,
        preferred_element_type=jnp.float32,
    )
    query_raw = split_heads(mixed[:, :D])
    key_raw = split_heads(mixed[:, D : 2 * D])
    query_heads = (query_raw * cosine + rotate_half(query_raw) * sine).astype(jnp.bfloat16)
    key_rows = join_heads(key_raw * cosine + rotate_half(key_raw) * sine).astype(jnp.bfloat16)
    value_rows = mixed[:, 2 * D :].astype(jnp.bfloat16)
    start_state = (
        jnp.full((HEADS, tok_rows), -1e30, jnp.float32),
        jnp.zeros((HEADS, tok_rows), jnp.float32),
        jnp.zeros((tok_rows, HEADS, HEAD_DIM), jnp.float32),
    )
    both_rows = lax.all_gather(
        jnp.concatenate([key_rows, value_rows], axis=-1), "ctx", axis=0, tiled=True
    )
    key_rows, value_rows = both_rows[:, :D], both_rows[:, D:]
    final_state = absorb(start_state, (key_rows, value_rows), query_heads)
    largest, running_sum, weighted = final_state
    attended = join_heads(weighted / running_sum.T[:, :, None])
    log_sums = (largest + jnp.log(running_sum)).T
    hidden = layer_in + jnp.dot(
        attended.astype(jnp.bfloat16), w_out, preferred_element_type=jnp.float32
    )
    normed_two, _ = normalize(hidden)
    gate_up = jnp.dot(
        (normed_two * gain_two.astype(jnp.float32)).astype(jnp.bfloat16),
        w_in,
        preferred_element_type=jnp.float32,
    )
    product = (jax.nn.gelu(gate_up[:, :FF], approximate=False) * gate_up[:, FF:]).astype(
        jnp.bfloat16
    )
    layer_out = hidden + jnp.dot(product, w_down, preferred_element_type=jnp.float32)
    return (
        layer_out,
        (layer_in, hidden, gate_up, query_heads, key_rows, value_rows, attended, log_sums),
    )


def backward_layer(upstream, cosine, sine, params, saved, cycle_place):
    gain_one, w_qkv, w_out, gain_two, w_in, w_down = params
    layer_in, hidden, gate_up, query_heads, key_rows, value_rows, attended, log_sums = saved
    scale_factor = HEAD_DIM ** (-0.5)
    tok_rows = upstream.shape[0]
    grad_branch = upstream.astype(jnp.bfloat16)
    gate_part = gate_up[:, :FF]
    up_part = gate_up[:, FF:]
    activated, gelu_pull = jax.vjp(
        lambda gate_in: jax.nn.gelu(gate_in, approximate=False), gate_part
    )
    product = (activated * up_part).astype(jnp.bfloat16)
    grad_down = jnp.einsum("tf,td->fd", product, grad_branch, preferred_element_type=jnp.float32)
    grad_product = jnp.einsum("td,fd->tf", grad_branch, w_down, preferred_element_type=jnp.float32)
    grad_gate = gelu_pull(grad_product * up_part)[0]
    grad_gate_up = jnp.concatenate([grad_gate, grad_product * activated], axis=-1).astype(
        jnp.bfloat16
    )
    normed_two, inverse_two = normalize(hidden)
    gain_two_full = gain_two.astype(jnp.float32)
    grad_in = jnp.einsum(
        "td,tf->df",
        (normed_two * gain_two_full).astype(jnp.bfloat16),
        grad_gate_up,
        preferred_element_type=jnp.float32,
    )
    grad_normed_two = jnp.einsum(
        "tf,df->td", grad_gate_up, w_in, preferred_element_type=jnp.float32
    )
    grad_gain_two = jnp.sum(grad_normed_two * normed_two, axis=0)
    grad_hidden = upstream + norm_back(grad_normed_two * gain_two_full, normed_two, inverse_two)
    grad_attn_out = grad_hidden.astype(jnp.bfloat16)
    grad_out = jnp.einsum(
        "td,te->de",
        attended.astype(jnp.bfloat16),
        grad_attn_out,
        preferred_element_type=jnp.float32,
    )
    grad_attended = split_heads(
        jnp.einsum("te,de->td", grad_attn_out, w_out, preferred_element_type=jnp.float32).astype(
            jnp.bfloat16
        )
    )
    deltas = jnp.sum(grad_attended.astype(jnp.float32) * split_heads(attended), axis=-1)
    stats = jnp.concatenate([log_sums, deltas], axis=-1)
    stats_high = lax.reduce_precision(stats, 8, 7)
    packed = jnp.concatenate(
        [
            join_heads(query_heads),
            join_heads(grad_attended),
            stats_high.astype(jnp.bfloat16),
            (stats - stats_high).astype(jnp.bfloat16),
        ],
        axis=-1,
    )
    packed = lax.all_gather(packed, "ctx", axis=0, tiled=True)
    queries_all, grads_all = packed[:, :D], packed[:, D : 2 * D]
    stats_all = packed[:, 2 * D :].astype(jnp.float32)
    stats_all = stats_all[:, : 2 * HEADS] + stats_all[:, 2 * HEADS :]
    all_logs, all_deltas = stats_all[:, :HEADS], stats_all[:, HEADS:]
    empty_heads = jnp.zeros((tok_rows, HEADS, HEAD_DIM), jnp.float32)
    key_heads = split_heads(key_rows)
    value_heads = split_heads(value_rows)
    _, grad_scores = score_grads(
        query_heads, grad_attended, log_sums, deltas, key_heads, value_heads
    )
    grad_query = (
        jnp.einsum("hqk,khe->qhe", grad_scores, key_heads, preferred_element_type=jnp.float32)
        * scale_factor
    )
    own_start = cycle_place * tok_rows
    own_keys = split_heads(lax.dynamic_slice_in_dim(key_rows, own_start, tok_rows, 0))
    own_values = split_heads(lax.dynamic_slice_in_dim(value_rows, own_start, tok_rows, 0))
    total_rows = queries_all.shape[0]
    block_rows = min(1024, total_rows)
    block_count = total_rows // block_rows

    def query_block(running, pieces):
        block_queries, block_grads, block_logs, block_deltas = pieces
        key_part, value_part = key_value_terms(
            split_heads(block_queries),
            split_heads(block_grads),
            block_logs,
            block_deltas,
            own_keys,
            own_values,
        )
        return ((running[0] + key_part, running[1] + value_part), None)

    stacked = (
        queries_all.reshape(block_count, block_rows, D),
        grads_all.reshape(block_count, block_rows, D),
        all_logs.reshape(block_count, block_rows, HEADS),
        all_deltas.reshape(block_count, block_rows, HEADS),
    )
    if block_count == 1:
        grad_key, grad_value_heads = key_value_terms(
            split_heads(queries_all),
            split_heads(grads_all),
            all_logs,
            all_deltas,
            own_keys,
            own_values,
        )
    else:
        (grad_key, grad_value_heads), _ = lax.scan(query_block, (empty_heads, empty_heads), stacked)
    grad_value = join_heads(grad_value_heads)
    query_grad_raw = grad_query * cosine + rotate_back(grad_query * sine)
    key_grad_raw = grad_key * cosine + rotate_back(grad_key * sine)
    grad_mixed = jnp.concatenate(
        [join_heads(query_grad_raw), join_heads(key_grad_raw), grad_value], axis=-1
    ).astype(jnp.bfloat16)
    normed_one, inverse_one = normalize(layer_in)
    gain_one_full = gain_one.astype(jnp.float32)
    grad_qkv = jnp.einsum(
        "td,tf->df",
        (normed_one * gain_one_full).astype(jnp.bfloat16),
        grad_mixed,
        preferred_element_type=jnp.float32,
    )
    grad_normed_one = jnp.einsum("tf,df->td", grad_mixed, w_qkv, preferred_element_type=jnp.float32)
    grad_gain_one = jnp.sum(grad_normed_one * normed_one, axis=0)
    grad_layer_in = grad_hidden + norm_back(
        grad_normed_one * gain_one_full, normed_one, inverse_one
    )
    return (grad_layer_in, (grad_gain_one, grad_qkv, grad_out, grad_gain_two, grad_in, grad_down))


def keep_slot(buffer, batch_slot, value, is_valid):
    previous = lax.dynamic_index_in_dim(buffer, batch_slot, 0, keepdims=False)
    return lax.dynamic_update_index_in_dim(
        buffer, jnp.where(is_valid, value, previous), batch_slot, 0
    )

MESH = pl.DeviceIdType.MESH


def greet(chips):
    me = lax.axis_index("ctx")
    chip, core = me // 2, me % 2
    w = lax.axis_index("wshard")
    barrier = pltpu.get_barrier_semaphore()
    peers = [{"ctx": ((chip + d) % chips) * 2 + core} for d in range(1, chips)]
    peers += [{"wshard": 1 - w}, {"ctx": chip * 2 + 1 - core}]
    for peer in peers:
        pl.semaphore_signal(barrier, inc=1, device_id=peer, device_id_type=MESH)
    pl.semaphore_wait(barrier, len(peers))


def gather_kernel(chips, count, *refs):
    ins, outs = refs[:count], refs[count : 2 * count]
    own_sem, z_send, z_recv, y_send, y_recv, c_send, c_recv = refs[2 * count :]
    me = lax.axis_index("ctx")
    chip, core = me // 2, me % 2
    w = lax.axis_index("wshard")

    def slot(chip_at, core_at, w_at):
        return (chip_at * 2 + core_at) * 2 + w_at

    greet(chips)
    own = slot(chip, core, w)

    def to_chip(a, d):
        return pltpu.make_async_remote_copy(
            ins[a].at[0], outs[a].at[own], z_send.at[a, d - 1], z_recv.at[a, d - 1],
            device_id={"ctx": ((chip + d) % chips) * 2 + core}, device_id_type=MESH)

    def to_wide(a, d):
        at = slot((chip - d + chips) % chips, core, w)
        source = ins[a].at[0] if d == 0 else outs[a].at[at]
        return pltpu.make_async_remote_copy(
            source, outs[a].at[at], y_send.at[a, d], y_recv.at[a, d],
            device_id={"wshard": 1 - w}, device_id_type=MESH)

    def to_core(a, d, far):
        at = slot((chip - d + chips) % chips, core, 1 - w if far else w)
        source = ins[a].at[0] if d == 0 and not far else outs[a].at[at]
        index = d + chips * far
        return pltpu.make_async_remote_copy(
            source, outs[a].at[at], c_send.at[a, index], c_recv.at[a, index],
            device_id={"ctx": chip * 2 + 1 - core}, device_id_type=MESH)

    def keep(a):
        return pltpu.make_async_copy(ins[a].at[0], outs[a].at[own], own_sem.at[a])

    for a in range(count):
        to_wide(a, 0).start()
        for d in range(1, chips):
            to_chip(a, d).start()
        to_core(a, 0, 0).start()
        keep(a).start()
    for a in range(count):
        for d in range(1, chips):
            to_chip(a, d).wait_recv()
            to_wide(a, d).start()
            to_core(a, d, 0).start()
        for d in range(chips):
            to_wide(a, d).wait_recv()
            to_core(a, d, 1).start()
    for a in range(count):
        keep(a).wait()
        for d in range(chips):
            for far in range(2):
                to_core(a, d, far).wait_recv()
    for a in range(count):
        for d in range(1, chips):
            to_chip(a, d).wait_send()
        for d in range(chips):
            to_wide(a, d).wait_send()
            for far in range(2):
                to_core(a, d, far).wait_send()


def gather_shards(arrays, chips):
    count = len(arrays)
    shards = chips * 4
    return pl.pallas_call(
        lambda *refs: gather_kernel(chips, count, *refs),
        out_shape=[jax.ShapeDtypeStruct((shards,) + x.shape[1:], x.dtype) for x in arrays],
        in_specs=[pl.BlockSpec(memory_space=pl.ANY)] * count,
        out_specs=[pl.BlockSpec(memory_space=pl.ANY)] * count,
        scratch_shapes=[
            pltpu.SemaphoreType.DMA((count,)),
            pltpu.SemaphoreType.DMA((count, chips - 1)),
            pltpu.SemaphoreType.DMA((count, chips - 1)),
            pltpu.SemaphoreType.DMA((count, chips)),
            pltpu.SemaphoreType.DMA((count, chips)),
            pltpu.SemaphoreType.DMA((count, 2 * chips)),
            pltpu.SemaphoreType.DMA((count, 2 * chips)),
        ],
        compiler_params=pltpu.CompilerParams(collective_id=0, has_side_effects=True),
        name="gather_shards",
    )(*arrays)


def scatter_kernel(chips, count, *refs):
    ins, outs = refs[:count], refs[count : 2 * count]
    rest = refs[2 * count :]
    from_core, from_wide, from_chip = rest[:count], rest[count : 2 * count], rest[2 * count : 3 * count]
    half, near = rest[3 * count : 4 * count], rest[4 * count : 5 * count]
    c_send, c_recv, y_send, y_recv, z_send, z_recv = rest[5 * count :]
    me = lax.axis_index("ctx")
    chip, core = me // 2, me % 2
    w = lax.axis_index("wshard")

    def slot(chip_at, core_at, w_at):
        return (chip_at * 2 + core_at) * 2 + w_at

    def wide(value):
        return value.astype(jnp.float32)

    greet(chips)

    def to_core(a, d, far):
        at = slot((chip + d) % chips, 1 - core, 1 - w if far else w)
        return pltpu.make_async_remote_copy(
            ins[a].at[at], from_core[a].at[d, far], c_send.at[a, d, far], c_recv.at[a, d, far],
            device_id={"ctx": chip * 2 + 1 - core}, device_id_type=MESH)

    def to_wide(a, d):
        return pltpu.make_async_remote_copy(
            half[a].at[d], from_wide[a].at[d], y_send.at[a, d], y_recv.at[a, d],
            device_id={"wshard": 1 - w}, device_id_type=MESH)

    def to_chip(a, d):
        return pltpu.make_async_remote_copy(
            near[a].at[d - 1], from_chip[a].at[d - 1], z_send.at[a, d - 1], z_recv.at[a, d - 1],
            device_id={"ctx": ((chip + d) % chips) * 2 + core}, device_id_type=MESH)

    order = list(range(1, chips)) + [0]
    for far in (1, 0):
        for a in range(count):
            for d in order:
                to_core(a, d, far).start()
    for a in range(count):
        for d in order:
            to_core(a, d, 1).wait_recv()
            mine = ins[a][slot((chip + d) % chips, core, 1 - w)]
            half[a][d] = (wide(mine) + wide(from_core[a][d, 1])).astype(jnp.bfloat16)
            to_wide(a, d).start()
    for a in range(count):
        for d in order:
            to_core(a, d, 0).wait_recv()
            to_wide(a, d).wait_recv()
            mine = ins[a][slot((chip + d) % chips, core, w)]
            total = wide(mine) + wide(from_core[a][d, 0]) + wide(from_wide[a][d])
            if d == 0:
                outs[a][0] = total
            else:
                near[a][d - 1] = total.astype(jnp.bfloat16)
                to_chip(a, d).start()
    for a in range(count):
        total = outs[a][0]
        for d in range(1, chips):
            to_chip(a, d).wait_recv()
            total = total + wide(from_chip[a][d - 1])
        outs[a][0] = total
    for a in range(count):
        for d in range(chips):
            to_core(a, d, 0).wait_send()
            to_core(a, d, 1).wait_send()
            to_wide(a, d).wait_send()
            if d:
                to_chip(a, d).wait_send()


def scatter_sums(arrays, chips):
    count = len(arrays)
    tails = [x.shape[1:] for x in arrays]

    def slots(*lead):
        return [pltpu.VMEM(lead + tail, jnp.bfloat16) for tail in tails]

    return pl.pallas_call(
        lambda *refs: scatter_kernel(chips, count, *refs),
        out_shape=[jax.ShapeDtypeStruct((1,) + tail, jnp.float32) for tail in tails],
        in_specs=[pl.BlockSpec(memory_space=pltpu.VMEM)] * count,
        out_specs=[pl.BlockSpec(memory_space=pltpu.VMEM)] * count,
        scratch_shapes=slots(chips, 2) + slots(chips) + slots(chips - 1) + slots(chips) + slots(chips - 1)
        + [
            pltpu.SemaphoreType.DMA((count, chips, 2)),
            pltpu.SemaphoreType.DMA((count, chips, 2)),
            pltpu.SemaphoreType.DMA((count, chips)),
            pltpu.SemaphoreType.DMA((count, chips)),
            pltpu.SemaphoreType.DMA((count, chips - 1)),
            pltpu.SemaphoreType.DMA((count, chips - 1)),
        ],
        compiler_params=pltpu.CompilerParams(
            collective_id=1, has_side_effects=True, vmem_limit_bytes=48 * 1024 * 1024
        ),
        name="scatter_sums",
    )(*arrays)


def use_kernels():
    cycle, wides = lax.axis_size("ctx"), lax.axis_size("wshard")
    return wides == 2 and cycle % 2 == 0 and 4 <= cycle <= 8


def gather_params(attn_gain, qkv_weight, out_weight, mlp_gain, in_weight, down_weight):
    chips = lax.axis_size("ctx") // 2
    gain_width = attn_gain.shape[1]
    gains = jnp.concatenate([attn_gain, mlp_gain], axis=0)
    gains = jnp.pad(gains, ((0, 14), (0, 128 - gain_width)))[None]
    gains, qkv, out, into, down = gather_shards(
        (gains, qkv_weight, out_weight, in_weight, down_weight), chips
    )
    return (
        gains[:, 0, :gain_width].reshape(D),
        qkv.reshape(D, -1),
        out.reshape(D, -1),
        gains[:, 1, :gain_width].reshape(D),
        into.reshape(D, -1),
        down.reshape(-1, D),
    )


def scatter_grads(summed):
    shards = lax.axis_size("ctx") * 2
    gain_one, qkv, out, gain_two, into, down = summed
    gain_width = gain_one.shape[0] // shards
    gains = jnp.stack([gain_one.reshape(shards, gain_width), gain_two.reshape(shards, gain_width)], axis=1)
    gains = jnp.pad(gains, ((0, 0), (0, 14), (0, 128 - gain_width)))
    parts = [x.reshape(shards, x.shape[0] // shards, x.shape[1]) for x in (down, into, out, qkv)]
    parts = [x.astype(jnp.bfloat16) for x in [gains] + parts]
    gains, down, into, out, qkv = scatter_sums(parts, shards // 4)
    return (gains[:, 0, :gain_width], qkv, out, gains[:, 1, :gain_width], into, down)


def staged_body(
    tokens,
    block_order,
    cotangent,
    attn_gain,
    qkv_weight,
    out_weight,
    mlp_gain,
    in_weight,
    down_weight,
):
    if use_kernels():
        params = gather_params(
            attn_gain, qkv_weight, out_weight, mlp_gain, in_weight, down_weight
        )
    else:
        gathered = (
            lax.all_gather(attn_gain, ("ctx", "wshard"), axis=1, tiled=True),
            lax.all_gather(qkv_weight, ("ctx", "wshard"), axis=1, tiled=True),
            lax.all_gather(out_weight, ("ctx", "wshard"), axis=1, tiled=True),
            lax.all_gather(mlp_gain, ("ctx", "wshard"), axis=1, tiled=True),
            lax.all_gather(in_weight, ("ctx", "wshard"), axis=1, tiled=True),
            lax.all_gather(down_weight, ("ctx", "wshard"), axis=1, tiled=True),
        )
        params = tuple((whole[0] for whole in gathered))
    section_id = lax.axis_index("section")
    section_count = lax.axis_size("section")
    cycle_place = lax.axis_index("ctx")
    micro_count = tokens.shape[0]
    tok_rows = tokens.shape[2]
    tick_count = micro_count + section_count - 1
    received = jnp.zeros((tok_rows, D), jnp.bfloat16)
    section_outs = jnp.zeros((micro_count, tok_rows, D), jnp.bfloat16)
    saved_all = None
    for tick in range(tick_count):
        batch_index = tick - section_id
        is_valid = (batch_index >= 0) & (batch_index < micro_count)
        batch_slot = jnp.clip(batch_index, 0, micro_count - 1)
        own_rows = tokens[batch_slot, 0]
        layer_in = jnp.where(section_id == 0, own_rows, received).astype(jnp.float32)
        cosine, sine = rotary(block_order[batch_slot, 0, cycle_place], tok_rows)
        layer_out, saved = forward_layer(layer_in, cosine, sine, params)
        if saved_all is None:
            saved_all = tuple(
                (jnp.zeros((micro_count,) + item.shape, item.dtype) for item in saved)
            )
        saved_all = tuple(
            (
                keep_slot(buffer, batch_slot, item, is_valid)
                for buffer, item in zip(saved_all, saved)
            )
        )
        outgoing = layer_out.astype(jnp.bfloat16)
        section_outs = keep_slot(section_outs, batch_slot, outgoing, is_valid)
        received = shifted(outgoing, "section", 1)
    grad_received = jnp.zeros((tok_rows, D), jnp.bfloat16)
    input_grads = jnp.zeros((micro_count, tok_rows, D), jnp.float32)
    summed = None
    for tick in range(tick_count):
        batch_index = tick - (section_count - 1 - section_id)
        is_valid = (batch_index >= 0) & (batch_index < micro_count)
        batch_slot = jnp.clip(batch_index, 0, micro_count - 1)
        upstream = jnp.where(
            section_id == section_count - 1, cotangent[batch_slot, 0], grad_received
        ).astype(jnp.float32)
        cosine, sine = rotary(block_order[batch_slot, 0, cycle_place], tok_rows)
        saved = tuple(
            (
                lax.dynamic_index_in_dim(buffer, batch_slot, 0, keepdims=False)
                for buffer in saved_all
            )
        )
        grad_layer_in, raw_grads = backward_layer(
            upstream, cosine, sine, params, saved, cycle_place
        )
        weight_grads = tuple(
            (jnp.where(is_valid, grad_term, jnp.zeros_like(grad_term)) for grad_term in raw_grads)
        )
        outgoing = grad_layer_in.astype(jnp.bfloat16)
        kept_grad = jnp.where(section_id == 0, grad_layer_in, outgoing.astype(jnp.float32))
        input_grads = keep_slot(input_grads, batch_slot, kept_grad, is_valid)
        summed = (
            weight_grads
            if summed is None
            else tuple((left + right for left, right in zip(summed, weight_grads)))
        )
        grad_received = shifted(outgoing, "section", -1)
    if use_kernels():
        summed = scatter_grads(summed)
    else:
        raised = [grad_term[None] for grad_term in summed]
        summed = (
            lax.psum_scatter(raised[0], ("ctx", "wshard"), scatter_dimension=1, tiled=True),
            lax.psum_scatter(raised[1], ("ctx", "wshard"), scatter_dimension=1, tiled=True),
            lax.psum_scatter(raised[2], ("ctx", "wshard"), scatter_dimension=1, tiled=True),
            lax.psum_scatter(raised[3], ("ctx", "wshard"), scatter_dimension=1, tiled=True),
            lax.psum_scatter(raised[4], ("ctx", "wshard"), scatter_dimension=1, tiled=True),
            lax.psum_scatter(raised[5], ("ctx", "wshard"), scatter_dimension=1, tiled=True),
        )
    return (
        section_outs[None, :, None],
        input_grads[None, :, None],
        summed[0],
        summed[1],
        summed[2],
        summed[3],
        summed[4],
        summed[5],
    )


def swap_kernel(cycle, in_ref, out_ref, own_sem, send, recv):
    me = lax.axis_index("ctx")
    barrier = pltpu.get_barrier_semaphore()
    peers = [lax.rem(me + d, cycle) for d in range(1, cycle)]
    for peer in peers:
        pl.semaphore_signal(barrier, inc=1, device_id={"ctx": peer}, device_id_type=MESH)
    pl.semaphore_wait(barrier, cycle - 1)
    copies = [
        pltpu.make_async_remote_copy(
            in_ref.at[peer], out_ref.at[me], send.at[index], recv.at[index],
            device_id={"ctx": peer}, device_id_type=MESH)
        for index, peer in enumerate(peers)
    ]
    for copy in copies:
        copy.start()
    own = pltpu.make_async_copy(in_ref.at[me], out_ref.at[me], own_sem)
    own.start()
    own.wait()
    for copy in copies:
        copy.wait()


def swap(pieces, collective):
    cycle = pieces.shape[0]
    return pl.pallas_call(
        lambda *refs: swap_kernel(cycle, *refs),
        out_shape=jax.ShapeDtypeStruct(pieces.shape, pieces.dtype),
        in_specs=[pl.BlockSpec(memory_space=pl.ANY)],
        out_specs=pl.BlockSpec(memory_space=pl.ANY),
        scratch_shapes=[
            pltpu.SemaphoreType.DMA,
            pltpu.SemaphoreType.DMA((cycle - 1,)),
            pltpu.SemaphoreType.DMA((cycle - 1,)),
        ],
        compiler_params=pltpu.CompilerParams(collective_id=collective, has_side_effects=True),
        name="swap_narrow" if collective == 2 else "swap_wide",
    )(pieces)


def dot_last(left, right):
    return lax.dot_general(left, right, (((1,), (1,)), ((), ())), preferred_element_type=jnp.float32)


def dot_first(left, right):
    return lax.dot_general(left, right, (((0,), (0,)), ((), ())), preferred_element_type=jnp.float32)


def attend_kernel(width, block, rows_ref, out_ref):
    start = pl.multiple_of(pl.program_id(0) * block, block)
    for low in range(0, width, HEAD_DIM):
        query = rows_ref[pl.ds(start, block), low : low + HEAD_DIM]
        key = rows_ref[:, width + low : width + low + HEAD_DIM]
        value = rows_ref[:, 2 * width + low : 2 * width + low + HEAD_DIM]
        scores = dot_last(query, key) * HEAD_DIM ** (-0.5)
        exponents = jnp.exp(scores - jnp.max(scores, axis=-1, keepdims=True))
        total = jnp.sum(exponents, axis=-1, keepdims=True)
        weighted = jnp.dot(exponents.astype(jnp.bfloat16), value, preferred_element_type=jnp.float32)
        out_ref[:, low : low + HEAD_DIM] = (weighted / total).astype(jnp.bfloat16)


def attend_rows(rows):
    length, width = rows.shape[0], rows.shape[1] // 3
    block = min(256, length)
    return pl.pallas_call(
        lambda *refs: attend_kernel(width, block, *refs),
        grid=(length // block,),
        out_shape=jax.ShapeDtypeStruct((length, width), jnp.bfloat16),
        in_specs=[pl.BlockSpec(rows.shape, lambda i: (0, 0))],
        out_specs=pl.BlockSpec((block, width), lambda i: (i, 0)),
        compiler_params=pltpu.CompilerParams(vmem_limit_bytes=48 * 1024 * 1024),
        name="attend_rows",
    )(rows)


def attend_back_kernel(width, block, steps, rows_ref, grad_ref, out_ref, key_sum, value_sum):
    step = pl.program_id(0)
    start = pl.multiple_of(step * block, block)

    @pl.when(step == 0)
    def _():
        key_sum[...] = jnp.zeros_like(key_sum)
        value_sum[...] = jnp.zeros_like(value_sum)

    scale = HEAD_DIM ** (-0.5)
    for low in range(0, width, HEAD_DIM):
        high = low + HEAD_DIM
        query = rows_ref[pl.ds(start, block), low:high]
        grad = grad_ref[pl.ds(start, block), low:high]
        key = rows_ref[:, width + low : width + high]
        value = rows_ref[:, 2 * width + low : 2 * width + high]
        scores = dot_last(query, key) * scale
        exponents = jnp.exp(scores - jnp.max(scores, axis=-1, keepdims=True))
        probs = exponents * (1.0 / jnp.sum(exponents, axis=-1, keepdims=True))
        upstream = dot_last(grad, value)
        delta = jnp.sum(probs * upstream, axis=-1, keepdims=True)
        grad_scores = (probs * (upstream - delta)).astype(jnp.bfloat16)
        query_grad = jnp.dot(grad_scores, key, preferred_element_type=jnp.float32) * scale
        out_ref[pl.ds(start, block), low:high] = query_grad.astype(jnp.bfloat16)
        key_sum[:, low:high] += dot_first(grad_scores, query)
        value_sum[:, low:high] += dot_first(probs.astype(jnp.bfloat16), grad)

    @pl.when(step == steps - 1)
    def _():
        out_ref[:, width : 2 * width] = (key_sum[...] * scale).astype(jnp.bfloat16)
        out_ref[:, 2 * width :] = value_sum[...].astype(jnp.bfloat16)


def attend_back(rows, grads):
    length, width = grads.shape
    block = min(256, length)
    steps = length // block
    return pl.pallas_call(
        lambda *refs: attend_back_kernel(width, block, steps, *refs),
        grid=(steps,),
        out_shape=jax.ShapeDtypeStruct(rows.shape, jnp.bfloat16),
        in_specs=[
            pl.BlockSpec(rows.shape, lambda i: (0, 0)),
            pl.BlockSpec(grads.shape, lambda i: (0, 0)),
        ],
        out_specs=pl.BlockSpec(rows.shape, lambda i: (0, 0)),
        scratch_shapes=[pltpu.VMEM(grads.shape, jnp.float32), pltpu.VMEM(grads.shape, jnp.float32)],
        compiler_params=pltpu.CompilerParams(vmem_limit_bytes=48 * 1024 * 1024),
        name="attend_back",
    )(rows, grads)


def to_units(values, micro, cycle):
    groups = cycle // micro
    rows, kinds = values.shape[0] // micro, values.shape[1] // D
    parts = values.reshape(micro, rows, kinds, groups, D // groups)
    return parts.transpose(0, 3, 1, 2, 4).reshape(cycle, rows, kinds * D // groups)


def from_units(pieces, micro):
    cycle, rows, width = pieces.shape
    groups = cycle // micro
    kinds = width * groups // D
    parts = pieces.reshape(micro, groups, rows, kinds, D // groups)
    return parts.transpose(0, 2, 3, 1, 4).reshape(micro * rows, kinds * D)


def to_sequence(values, micro, cycle):
    kinds = values.shape[1] // D
    received = swap(to_units(values, micro, cycle), 2 if kinds == 1 else 3)
    return received.reshape(-1, received.shape[2])


def from_sequence(rows, micro, cycle):
    kinds = 2 if rows.shape[1] * cycle // micro == D else 3
    received = swap(rows.reshape(cycle, -1, rows.shape[1]), kinds)
    return from_units(received, micro)


def halves(values):
    half_width = HEAD_DIM // 2
    first = lax.broadcasted_iota(jnp.int32, values.shape, 1) % HEAD_DIM < half_width
    return (first, jnp.roll(values, -half_width, axis=1), jnp.roll(values, half_width, axis=1))


def turn(values):
    first, ahead, behind = halves(values)
    return jnp.where(first, -ahead, behind)


def turn_back(values):
    first, ahead, behind = halves(values)
    return jnp.where(first, ahead, -behind)


def fast_forward(layer_in, cosine, sine, params, micro, cycle):
    gain_one, w_qkv, w_out, gain_two, w_in, w_down = params
    normed_one, _ = normalize(layer_in)
    mixed = jnp.dot(
        (normed_one * gain_one.astype(jnp.float32)).astype(jnp.bfloat16),
        w_qkv,
        preferred_element_type=jnp.float32,
    )
    rotated = mixed[:, : 2 * D]
    rotated = rotated * cosine + turn(rotated) * sine
    mixed = jnp.concatenate([rotated, mixed[:, 2 * D :]], axis=-1).astype(jnp.bfloat16)
    rows = to_sequence(mixed, micro, cycle)
    attended = from_sequence(attend_rows(rows), micro, cycle)
    hidden = layer_in + jnp.dot(attended, w_out, preferred_element_type=jnp.float32)
    normed_two, _ = normalize(hidden)
    gate_up = jnp.dot(
        (normed_two * gain_two.astype(jnp.float32)).astype(jnp.bfloat16),
        w_in,
        preferred_element_type=jnp.float32,
    )
    product = (jax.nn.gelu(gate_up[:, :FF], approximate=False) * gate_up[:, FF:]).astype(
        jnp.bfloat16
    )
    layer_out = hidden + jnp.dot(product, w_down, preferred_element_type=jnp.float32)
    return (layer_out, (layer_in, hidden, gate_up, rows, attended))


def fast_backward(upstream, cosine, sine, params, saved, micro, cycle):
    gain_one, w_qkv, w_out, gain_two, w_in, w_down = params
    layer_in, hidden, gate_up, rows, attended = saved
    grad_branch = upstream.astype(jnp.bfloat16)
    up_part = gate_up[:, FF:]
    activated, gelu_pull = jax.vjp(
        lambda gate_in: jax.nn.gelu(gate_in, approximate=False), gate_up[:, :FF]
    )
    product = (activated * up_part).astype(jnp.bfloat16)
    grad_down = dot_first(product, grad_branch)
    grad_product = dot_last(grad_branch, w_down)
    grad_gate_up = jnp.concatenate(
        [gelu_pull(grad_product * up_part)[0], grad_product * activated], axis=-1
    ).astype(jnp.bfloat16)
    normed_two, inverse_two = normalize(hidden)
    gain_two_full = gain_two.astype(jnp.float32)
    grad_in = dot_first((normed_two * gain_two_full).astype(jnp.bfloat16), grad_gate_up)
    grad_normed_two = dot_last(grad_gate_up, w_in)
    grad_gain_two = jnp.sum(grad_normed_two * normed_two, axis=0)
    grad_hidden = upstream + norm_back(grad_normed_two * gain_two_full, normed_two, inverse_two)
    grad_attn_out = grad_hidden.astype(jnp.bfloat16)
    grad_out = dot_first(attended, grad_attn_out)
    grad_attended = dot_last(grad_attn_out, w_out).astype(jnp.bfloat16)
    grad_rows = attend_back(rows, to_sequence(grad_attended, micro, cycle))
    grad_raw = from_sequence(grad_rows, micro, cycle)
    rotated = grad_raw[:, : 2 * D].astype(jnp.float32)
    rotated = (rotated * cosine + turn_back(rotated * sine)).astype(jnp.bfloat16)
    grad_mixed = jnp.concatenate([rotated, grad_raw[:, 2 * D :]], axis=-1)
    normed_one, inverse_one = normalize(layer_in)
    gain_one_full = gain_one.astype(jnp.float32)
    grad_qkv = dot_first((normed_one * gain_one_full).astype(jnp.bfloat16), grad_mixed)
    grad_normed_one = dot_last(grad_mixed, w_qkv)
    grad_gain_one = jnp.sum(grad_normed_one * normed_one, axis=0)
    grad_layer_in = grad_hidden + norm_back(
        grad_normed_one * gain_one_full, normed_one, inverse_one
    )
    return (grad_layer_in, (grad_gain_one, grad_qkv, grad_out, grad_gain_two, grad_in, grad_down))


def fast_body(tokens, block_order, cotangent, *weights):
    section_id = lax.axis_index("section")
    section_count = lax.axis_size("section")
    cycle = lax.axis_size("ctx")
    micro, _, tok_rows, _ = tokens.shape
    params = gather_params(*weights)
    blocks = block_order[:, 0, lax.axis_index("ctx")]
    tables = [rotary(blocks[index], tok_rows) for index in range(micro)]
    cosine, sine = (
        jnp.tile(jnp.concatenate([table[kind][:, 0] for table in tables], axis=0), (1, 2 * HEADS))
        for kind in range(2)
    )
    own_rows = tokens[:, 0].reshape(micro * tok_rows, D)
    upstream_rows = cotangent[:, 0].reshape(micro * tok_rows, D)
    layer_in = own_rows
    for tick in range(section_count):
        layer_out, saved = fast_forward(
            layer_in.astype(jnp.float32), cosine, sine, params, micro, cycle
        )
        outgoing = layer_out.astype(jnp.bfloat16)
        if tick < section_count - 1:
            layer_in = jnp.where(section_id == 0, own_rows, shifted(outgoing, "section", 1))
    section_outs = outgoing
    upstream = upstream_rows
    for tick in range(section_count):
        grad_layer_in, summed = fast_backward(
            upstream.astype(jnp.float32), cosine, sine, params, saved, micro, cycle
        )
        outgoing = grad_layer_in.astype(jnp.bfloat16)
        if tick < section_count - 1:
            upstream = jnp.where(
                section_id == section_count - 1, upstream_rows, shifted(outgoing, "section", -1)
            )
    input_grads = jnp.where(section_id == 0, grad_layer_in, outgoing.astype(jnp.float32))
    shape = (1, micro, 1, tok_rows, D)
    return (section_outs.reshape(shape), input_grads.reshape(shape)) + scatter_grads(summed)


def body(tokens, *rest):
    micro, cycle = tokens.shape[0], lax.axis_size("ctx")
    if use_kernels() and cycle % micro == 0 and HEADS % (cycle // micro) == 0:
        return fast_body(tokens, *rest)
    return staged_body(tokens, *rest)


def solution(mesh):
    in_specs = (
        P(None, "wshard", "ctx", None),
        P(None, "wshard", None),
        P(None, "wshard", "ctx", None),
        P("section", ("ctx", "wshard")),
        P("section", ("ctx", "wshard"), None),
        P("section", ("ctx", "wshard"), None),
        P("section", ("ctx", "wshard")),
        P("section", ("ctx", "wshard"), None),
        P("section", ("ctx", "wshard"), None),
    )
    out_specs = (
        P("section", None, "wshard", "ctx", None),
        P("section", None, "wshard", "ctx", None),
        P("section", ("ctx", "wshard")),
        P("section", ("ctx", "wshard"), None),
        P("section", ("ctx", "wshard"), None),
        P("section", ("ctx", "wshard")),
        P("section", ("ctx", "wshard"), None),
        P("section", ("ctx", "wshard"), None),
    )
    return jax.shard_map(body, mesh=mesh, in_specs=in_specs, out_specs=out_specs, check_vma=False)
```

```python
import jax
import jax.numpy as jnp
from jax import lax
from jax.experimental import pallas as pl
from jax.experimental.pallas import tpu as pltpu
from jax.sharding import PartitionSpec as P

D = 768
HEADS = 12
HEAD_DIM = 64
FF = 1152


epsilon = 1e-05
rope_base = 160000.0


def shifted(x, axis, by):
    peers = lax.axis_size(axis)
    pairs = [(i, i + by) for i in range(peers) if 0 <= i + by < peers]
    return lax.ppermute(x, axis, pairs)


def normalize(values):
    row_mean = jnp.mean(values, axis=-1, keepdims=True)
    centered = values - row_mean
    variance = jnp.mean(centered * centered, axis=-1, keepdims=True)
    inverse = lax.rsqrt(variance + epsilon)
    return (centered * inverse, inverse)


def norm_back(grad_hat, normed, inverse):
    first_mean = jnp.mean(grad_hat, axis=-1, keepdims=True)
    second_mean = jnp.mean(grad_hat * normed, axis=-1, keepdims=True)
    return (grad_hat - first_mean - normed * second_mean) * inverse


def split_heads(values):
    return values.reshape(values.shape[0], HEADS, HEAD_DIM)


def join_heads(values):
    return values.reshape(values.shape[0], HEADS * HEAD_DIM)


def rotate_half(values):
    half_width = values.shape[-1] // 2
    return jnp.concatenate([-values[..., half_width:], values[..., :half_width]], axis=-1)


def rotate_back(values):
    half_width = values.shape[-1] // 2
    return jnp.concatenate([values[..., half_width:], -values[..., :half_width]], axis=-1)


def rotary(block_id, tok_rows):
    positions = (block_id * tok_rows + jnp.arange(tok_rows, dtype=jnp.int32)).astype(jnp.float32)
    inverse = 1.0 / rope_base ** (jnp.arange(0, HEAD_DIM, 2, dtype=jnp.float32) / HEAD_DIM)
    angles = positions[:, None] * inverse[None, :]
    cosine = jnp.concatenate([jnp.cos(angles), jnp.cos(angles)], axis=-1)[:, None, :]
    sine = jnp.concatenate([jnp.sin(angles), jnp.sin(angles)], axis=-1)[:, None, :]
    return (cosine, sine)


def absorb(state_now, arrived, query_heads):
    largest, running_sum, weighted = state_now
    key_rows, value_rows = arrived
    scores = jnp.einsum(
        "qhe,khe->hqk", query_heads, split_heads(key_rows), preferred_element_type=jnp.float32
    ) * HEAD_DIM ** (-0.5)
    new_max = jnp.maximum(largest, jnp.max(scores, axis=-1))
    shrink = jnp.exp(largest - new_max)
    exponents = jnp.exp(scores - new_max[:, :, None])
    running_sum = jnp.sum(exponents, axis=-1)
    weighted = weighted * shrink.T[:, :, None] + jnp.einsum(
        "hqk,khe->qhe",
        exponents.astype(jnp.bfloat16),
        split_heads(value_rows),
        preferred_element_type=jnp.float32,
    )
    return (new_max, running_sum, weighted)


def score_grads(query_heads, grad_heads, log_sums, deltas, key_heads, value_heads):
    scores = jnp.einsum(
        "qhe,khe->hqk", query_heads, key_heads, preferred_element_type=jnp.float32
    ) * HEAD_DIM ** (-0.5)
    weights = jnp.exp(scores - log_sums.T[:, :, None])
    upstream = jnp.einsum(
        "qhe,khe->hqk", grad_heads, value_heads, preferred_element_type=jnp.float32
    )
    grad_scores = (weights * (upstream - deltas.T[:, :, None])).astype(jnp.bfloat16)
    return (weights.astype(jnp.bfloat16), grad_scores)


def key_value_terms(query_heads, grad_heads, log_sums, deltas, key_heads, value_heads):
    weights_low, grad_scores = score_grads(
        query_heads, grad_heads, log_sums, deltas, key_heads, value_heads
    )
    key_part = jnp.einsum(
        "hqk,qhe->khe", grad_scores, query_heads, preferred_element_type=jnp.float32
    ) * HEAD_DIM ** (-0.5)
    value_part = jnp.einsum(
        "hqk,qhe->khe", weights_low, grad_heads, preferred_element_type=jnp.float32
    )
    return (key_part, value_part)


def forward_layer(layer_in, cosine, sine, params):
    gain_one, w_qkv, w_out, gain_two, w_in, w_down = params
    tok_rows = layer_in.shape[0]
    normed_one, _ = normalize(layer_in)
    mixed = jnp.dot(
        (normed_one * gain_one.astype(jnp.float32)).astype(jnp.bfloat16),
        w_qkv,
        preferred_element_type=jnp.float32,
    )
    query_raw = split_heads(mixed[:, :D])
    key_raw = split_heads(mixed[:, D : 2 * D])
    query_heads = (query_raw * cosine + rotate_half(query_raw) * sine).astype(jnp.bfloat16)
    key_rows = join_heads(key_raw * cosine + rotate_half(key_raw) * sine).astype(jnp.bfloat16)
    value_rows = mixed[:, 2 * D :].astype(jnp.bfloat16)
    start_state = (
        jnp.full((HEADS, tok_rows), -1e30, jnp.float32),
        jnp.zeros((HEADS, tok_rows), jnp.float32),
        jnp.zeros((tok_rows, HEADS, HEAD_DIM), jnp.float32),
    )
    both_rows = lax.all_gather(
        jnp.concatenate([key_rows, value_rows], axis=-1), "ctx", axis=0, tiled=True
    )
    key_rows, value_rows = both_rows[:, :D], both_rows[:, D:]
    final_state = absorb(start_state, (key_rows, value_rows), query_heads)
    largest, running_sum, weighted = final_state
    attended = join_heads(weighted / running_sum.T[:, :, None])
    log_sums = (largest + jnp.log(running_sum)).T
    hidden = layer_in + jnp.dot(
        attended.astype(jnp.bfloat16), w_out, preferred_element_type=jnp.float32
    )
    normed_two, _ = normalize(hidden)
    gate_up = jnp.dot(
        (normed_two * gain_two.astype(jnp.float32)).astype(jnp.bfloat16),
        w_in,
        preferred_element_type=jnp.float32,
    )
    product = (jax.nn.gelu(gate_up[:, :FF], approximate=False) * gate_up[:, FF:]).astype(
        jnp.bfloat16
    )
    layer_out = hidden + jnp.dot(product, w_down, preferred_element_type=jnp.float32)
    return (
        layer_out,
        (layer_in, hidden, gate_up, query_heads, key_rows, value_rows, attended, log_sums),
    )


def backward_layer(upstream, cosine, sine, params, saved, cycle_place):
    gain_one, w_qkv, w_out, gain_two, w_in, w_down = params
    layer_in, hidden, gate_up, query_heads, key_rows, value_rows, attended, log_sums = saved
    scale_factor = HEAD_DIM ** (-0.5)
    tok_rows = upstream.shape[0]
    grad_branch = upstream.astype(jnp.bfloat16)
    gate_part = gate_up[:, :FF]
    up_part = gate_up[:, FF:]
    activated, gelu_pull = jax.vjp(
        lambda gate_in: jax.nn.gelu(gate_in, approximate=False), gate_part
    )
    product = (activated * up_part).astype(jnp.bfloat16)
    grad_down = jnp.einsum("tf,td->fd", product, grad_branch, preferred_element_type=jnp.float32)
    grad_product = jnp.einsum("td,fd->tf", grad_branch, w_down, preferred_element_type=jnp.float32)
    grad_gate = gelu_pull(grad_product * up_part)[0]
    grad_gate_up = jnp.concatenate([grad_gate, grad_product * activated], axis=-1).astype(
        jnp.bfloat16
    )
    normed_two, inverse_two = normalize(hidden)
    gain_two_full = gain_two.astype(jnp.float32)
    grad_in = jnp.einsum(
        "td,tf->df",
        (normed_two * gain_two_full).astype(jnp.bfloat16),
        grad_gate_up,
        preferred_element_type=jnp.float32,
    )
    grad_normed_two = jnp.einsum(
        "tf,df->td", grad_gate_up, w_in, preferred_element_type=jnp.float32
    )
    grad_gain_two = jnp.sum(grad_normed_two * normed_two, axis=0)
    grad_hidden = upstream + norm_back(grad_normed_two * gain_two_full, normed_two, inverse_two)
    grad_attn_out = grad_hidden.astype(jnp.bfloat16)
    grad_out = jnp.einsum(
        "td,te->de",
        attended.astype(jnp.bfloat16),
        grad_attn_out,
        preferred_element_type=jnp.float32,
    )
    grad_attended = split_heads(
        jnp.einsum("te,de->td", grad_attn_out, w_out, preferred_element_type=jnp.float32).astype(
            jnp.bfloat16
        )
    )
    deltas = jnp.sum(grad_attended.astype(jnp.float32) * split_heads(attended), axis=-1)
    stats = jnp.concatenate([log_sums, deltas], axis=-1)
    stats_high = lax.reduce_precision(stats, 8, 7)
    packed = jnp.concatenate(
        [
            join_heads(query_heads),
            join_heads(grad_attended),
            stats_high.astype(jnp.bfloat16),
            (stats - stats_high).astype(jnp.bfloat16),
        ],
        axis=-1,
    )
    packed = lax.all_gather(packed, "ctx", axis=0, tiled=True)
    queries_all, grads_all = packed[:, :D], packed[:, D : 2 * D]
    stats_all = packed[:, 2 * D :].astype(jnp.float32)
    stats_all = stats_all[:, : 2 * HEADS] + stats_all[:, 2 * HEADS :]
    all_logs, all_deltas = stats_all[:, :HEADS], stats_all[:, HEADS:]
    empty_heads = jnp.zeros((tok_rows, HEADS, HEAD_DIM), jnp.float32)
    key_heads = split_heads(key_rows)
    value_heads = split_heads(value_rows)
    _, grad_scores = score_grads(
        query_heads, grad_attended, log_sums, deltas, key_heads, value_heads
    )
    grad_query = (
        jnp.einsum("hqk,khe->qhe", grad_scores, key_heads, preferred_element_type=jnp.float32)
        * scale_factor
    )
    own_start = cycle_place * tok_rows
    own_keys = split_heads(lax.dynamic_slice_in_dim(key_rows, own_start, tok_rows, 0))
    own_values = split_heads(lax.dynamic_slice_in_dim(value_rows, own_start, tok_rows, 0))
    total_rows = queries_all.shape[0]
    block_rows = min(1024, total_rows)
    block_count = total_rows // block_rows

    def query_block(running, pieces):
        block_queries, block_grads, block_logs, block_deltas = pieces
        key_part, value_part = key_value_terms(
            split_heads(block_queries),
            split_heads(block_grads),
            block_logs,
            block_deltas,
            own_keys,
            own_values,
        )
        return ((running[0] + key_part, running[1] + value_part), None)

    stacked = (
        queries_all.reshape(block_count, block_rows, D),
        grads_all.reshape(block_count, block_rows, D),
        all_logs.reshape(block_count, block_rows, HEADS),
        all_deltas.reshape(block_count, block_rows, HEADS),
    )
    if block_count == 1:
        grad_key, grad_value_heads = key_value_terms(
            split_heads(queries_all),
            split_heads(grads_all),
            all_logs,
            all_deltas,
            own_keys,
            own_values,
        )
    else:
        (grad_key, grad_value_heads), _ = lax.scan(query_block, (empty_heads, empty_heads), stacked)
    grad_value = join_heads(grad_value_heads)
    query_grad_raw = grad_query * cosine + rotate_back(grad_query * sine)
    key_grad_raw = grad_key * cosine + rotate_back(grad_key * sine)
    grad_mixed = jnp.concatenate(
        [join_heads(query_grad_raw), join_heads(key_grad_raw), grad_value], axis=-1
    ).astype(jnp.bfloat16)
    normed_one, inverse_one = normalize(layer_in)
    gain_one_full = gain_one.astype(jnp.float32)
    grad_qkv = jnp.einsum(
        "td,tf->df",
        (normed_one * gain_one_full).astype(jnp.bfloat16),
        grad_mixed,
        preferred_element_type=jnp.float32,
    )
    grad_normed_one = jnp.einsum("tf,df->td", grad_mixed, w_qkv, preferred_element_type=jnp.float32)
    grad_gain_one = jnp.sum(grad_normed_one * normed_one, axis=0)
    grad_layer_in = grad_hidden + norm_back(
        grad_normed_one * gain_one_full, normed_one, inverse_one
    )
    return (grad_layer_in, (grad_gain_one, grad_qkv, grad_out, grad_gain_two, grad_in, grad_down))


def keep_slot(buffer, batch_slot, value, is_valid):
    previous = lax.dynamic_index_in_dim(buffer, batch_slot, 0, keepdims=False)
    return lax.dynamic_update_index_in_dim(
        buffer, jnp.where(is_valid, value, previous), batch_slot, 0
    )

MESH = pl.DeviceIdType.MESH


def greet(chips):
    me = lax.axis_index("ctx")
    chip, core = me // 2, me % 2
    w = lax.axis_index("wshard")
    barrier = pltpu.get_barrier_semaphore()
    peers = [{"ctx": ((chip + d) % chips) * 2 + core} for d in range(1, chips)]
    peers += [{"wshard": 1 - w}, {"ctx": chip * 2 + 1 - core}]
    for peer in peers:
        pl.semaphore_signal(barrier, inc=1, device_id=peer, device_id_type=MESH)
    pl.semaphore_wait(barrier, len(peers))


def gather_kernel(chips, count, *refs):
    ins, outs = refs[:count], refs[count : 2 * count]
    own_sem, z_send, z_recv, y_send, y_recv, c_send, c_recv = refs[2 * count :]
    me = lax.axis_index("ctx")
    chip, core = me // 2, me % 2
    w = lax.axis_index("wshard")

    def slot(chip_at, core_at, w_at):
        return (chip_at * 2 + core_at) * 2 + w_at

    greet(chips)
    own = slot(chip, core, w)

    def to_chip(a, d):
        return pltpu.make_async_remote_copy(
            ins[a].at[0], outs[a].at[own], z_send.at[a, d - 1], z_recv.at[a, d - 1],
            device_id={"ctx": ((chip + d) % chips) * 2 + core}, device_id_type=MESH)

    def to_wide(a, d):
        at = slot((chip - d + chips) % chips, core, w)
        source = ins[a].at[0] if d == 0 else outs[a].at[at]
        return pltpu.make_async_remote_copy(
            source, outs[a].at[at], y_send.at[a, d], y_recv.at[a, d],
            device_id={"wshard": 1 - w}, device_id_type=MESH)

    def to_core(a, d, far):
        at = slot((chip - d + chips) % chips, core, 1 - w if far else w)
        source = ins[a].at[0] if d == 0 and not far else outs[a].at[at]
        index = d + chips * far
        return pltpu.make_async_remote_copy(
            source, outs[a].at[at], c_send.at[a, index], c_recv.at[a, index],
            device_id={"ctx": chip * 2 + 1 - core}, device_id_type=MESH)

    def keep(a):
        return pltpu.make_async_copy(ins[a].at[0], outs[a].at[own], own_sem.at[a])

    for a in range(count):
        to_wide(a, 0).start()
        for d in range(1, chips):
            to_chip(a, d).start()
        to_core(a, 0, 0).start()
        keep(a).start()
    for a in range(count):
        for d in range(1, chips):
            to_chip(a, d).wait_recv()
            to_wide(a, d).start()
            to_core(a, d, 0).start()
        for d in range(chips):
            to_wide(a, d).wait_recv()
            to_core(a, d, 1).start()
    for a in range(count):
        keep(a).wait()
        for d in range(chips):
            for far in range(2):
                to_core(a, d, far).wait_recv()
    for a in range(count):
        for d in range(1, chips):
            to_chip(a, d).wait_send()
        for d in range(chips):
            to_wide(a, d).wait_send()
            for far in range(2):
                to_core(a, d, far).wait_send()


def gather_shards(arrays, chips):
    count = len(arrays)
    shards = chips * 4
    return pl.pallas_call(
        lambda *refs: gather_kernel(chips, count, *refs),
        out_shape=[jax.ShapeDtypeStruct((shards,) + x.shape[1:], x.dtype) for x in arrays],
        in_specs=[pl.BlockSpec(memory_space=pl.ANY)] * count,
        out_specs=[pl.BlockSpec(memory_space=pl.ANY)] * count,
        scratch_shapes=[
            pltpu.SemaphoreType.DMA((count,)),
            pltpu.SemaphoreType.DMA((count, chips - 1)),
            pltpu.SemaphoreType.DMA((count, chips - 1)),
            pltpu.SemaphoreType.DMA((count, chips)),
            pltpu.SemaphoreType.DMA((count, chips)),
            pltpu.SemaphoreType.DMA((count, 2 * chips)),
            pltpu.SemaphoreType.DMA((count, 2 * chips)),
        ],
        compiler_params=pltpu.CompilerParams(collective_id=0, has_side_effects=True),
        name="gather_shards",
    )(*arrays)


def scatter_kernel(chips, count, *refs):
    ins, outs = refs[:count], refs[count : 2 * count]
    rest = refs[2 * count :]
    from_core, from_wide, from_chip = rest[:count], rest[count : 2 * count], rest[2 * count : 3 * count]
    half, near = rest[3 * count : 4 * count], rest[4 * count : 5 * count]
    c_send, c_recv, y_send, y_recv, z_send, z_recv = rest[5 * count :]
    me = lax.axis_index("ctx")
    chip, core = me // 2, me % 2
    w = lax.axis_index("wshard")

    def slot(chip_at, core_at, w_at):
        return (chip_at * 2 + core_at) * 2 + w_at

    def wide(value):
        return value.astype(jnp.float32)

    greet(chips)

    def to_core(a, d, far):
        at = slot((chip + d) % chips, 1 - core, 1 - w if far else w)
        return pltpu.make_async_remote_copy(
            ins[a].at[at], from_core[a].at[d, far], c_send.at[a, d, far], c_recv.at[a, d, far],
            device_id={"ctx": chip * 2 + 1 - core}, device_id_type=MESH)

    def to_wide(a, d):
        return pltpu.make_async_remote_copy(
            half[a].at[d], from_wide[a].at[d], y_send.at[a, d], y_recv.at[a, d],
            device_id={"wshard": 1 - w}, device_id_type=MESH)

    def to_chip(a, d):
        return pltpu.make_async_remote_copy(
            near[a].at[d - 1], from_chip[a].at[d - 1], z_send.at[a, d - 1], z_recv.at[a, d - 1],
            device_id={"ctx": ((chip + d) % chips) * 2 + core}, device_id_type=MESH)

    order = list(range(1, chips)) + [0]
    for far in (1, 0):
        for a in range(count):
            for d in order:
                to_core(a, d, far).start()
    for a in range(count):
        for d in order:
            to_core(a, d, 1).wait_recv()
            mine = ins[a][slot((chip + d) % chips, core, 1 - w)]
            half[a][d] = (wide(mine) + wide(from_core[a][d, 1])).astype(jnp.bfloat16)
            to_wide(a, d).start()
    for a in range(count):
        for d in order:
            to_core(a, d, 0).wait_recv()
            to_wide(a, d).wait_recv()
            mine = ins[a][slot((chip + d) % chips, core, w)]
            total = wide(mine) + wide(from_core[a][d, 0]) + wide(from_wide[a][d])
            if d == 0:
                outs[a][0] = total
            else:
                near[a][d - 1] = total.astype(jnp.bfloat16)
                to_chip(a, d).start()
    for a in range(count):
        total = outs[a][0]
        for d in range(1, chips):
            to_chip(a, d).wait_recv()
            total = total + wide(from_chip[a][d - 1])
        outs[a][0] = total
    for a in range(count):
        for d in range(chips):
            to_core(a, d, 0).wait_send()
            to_core(a, d, 1).wait_send()
            to_wide(a, d).wait_send()
            if d:
                to_chip(a, d).wait_send()


def scatter_sums(arrays, chips):
    count = len(arrays)
    tails = [x.shape[1:] for x in arrays]

    def slots(*lead):
        return [pltpu.VMEM(lead + tail, jnp.bfloat16) for tail in tails]

    return pl.pallas_call(
        lambda *refs: scatter_kernel(chips, count, *refs),
        out_shape=[jax.ShapeDtypeStruct((1,) + tail, jnp.float32) for tail in tails],
        in_specs=[pl.BlockSpec(memory_space=pltpu.VMEM)] * count,
        out_specs=[pl.BlockSpec(memory_space=pltpu.VMEM)] * count,
        scratch_shapes=slots(chips, 2) + slots(chips) + slots(chips - 1) + slots(chips) + slots(chips - 1)
        + [
            pltpu.SemaphoreType.DMA((count, chips, 2)),
            pltpu.SemaphoreType.DMA((count, chips, 2)),
            pltpu.SemaphoreType.DMA((count, chips)),
            pltpu.SemaphoreType.DMA((count, chips)),
            pltpu.SemaphoreType.DMA((count, chips - 1)),
            pltpu.SemaphoreType.DMA((count, chips - 1)),
        ],
        compiler_params=pltpu.CompilerParams(
            collective_id=1, has_side_effects=True, vmem_limit_bytes=48 * 1024 * 1024
        ),
        name="scatter_sums",
    )(*arrays)


def use_kernels():
    cycle, wides = lax.axis_size("ctx"), lax.axis_size("wshard")
    return wides == 2 and cycle % 2 == 0 and 4 <= cycle <= 8


def gather_params(attn_gain, qkv_weight, out_weight, mlp_gain, in_weight, down_weight):
    chips = lax.axis_size("ctx") // 2
    gain_width = attn_gain.shape[1]
    gains = jnp.concatenate([attn_gain, mlp_gain], axis=0)
    gains = jnp.pad(gains, ((0, 14), (0, 128 - gain_width)))[None]
    into = lax.all_gather(in_weight, ("ctx", "wshard"), axis=1, tiled=True)
    down = lax.all_gather(down_weight, ("ctx", "wshard"), axis=1, tiled=True)
    gains, qkv, out = gather_shards((gains, qkv_weight, out_weight), chips)
    return (
        gains[:, 0, :gain_width].reshape(D),
        qkv.reshape(D, -1),
        out.reshape(D, -1),
        gains[:, 1, :gain_width].reshape(D),
        into.reshape(D, -1),
        down.reshape(-1, D),
    )


def scatter_grads(summed):
    shards = lax.axis_size("ctx") * 2
    gain_one, qkv, out, gain_two, into, down = summed
    gain_width = gain_one.shape[0] // shards
    gains = jnp.stack([gain_one.reshape(shards, gain_width), gain_two.reshape(shards, gain_width)], axis=1)
    gains = jnp.pad(gains, ((0, 0), (0, 14), (0, 128 - gain_width)))
    parts = [x.reshape(shards, x.shape[0] // shards, x.shape[1]) for x in (down, into, out, qkv)]
    parts = [x.astype(jnp.bfloat16) for x in [gains] + parts]
    gains, down, into, out, qkv = scatter_sums(parts, shards // 4)
    return (gains[:, 0, :gain_width], qkv, out, gains[:, 1, :gain_width], into, down)


def staged_body(
    tokens,
    block_order,
    cotangent,
    attn_gain,
    qkv_weight,
    out_weight,
    mlp_gain,
    in_weight,
    down_weight,
):
    if use_kernels():
        params = gather_params(
            attn_gain, qkv_weight, out_weight, mlp_gain, in_weight, down_weight
        )
    else:
        gathered = (
            lax.all_gather(attn_gain, ("ctx", "wshard"), axis=1, tiled=True),
            lax.all_gather(qkv_weight, ("ctx", "wshard"), axis=1, tiled=True),
            lax.all_gather(out_weight, ("ctx", "wshard"), axis=1, tiled=True),
            lax.all_gather(mlp_gain, ("ctx", "wshard"), axis=1, tiled=True),
            lax.all_gather(in_weight, ("ctx", "wshard"), axis=1, tiled=True),
            lax.all_gather(down_weight, ("ctx", "wshard"), axis=1, tiled=True),
        )
        params = tuple((whole[0] for whole in gathered))
    section_id = lax.axis_index("section")
    section_count = lax.axis_size("section")
    cycle_place = lax.axis_index("ctx")
    micro_count = tokens.shape[0]
    tok_rows = tokens.shape[2]
    tick_count = micro_count + section_count - 1
    received = jnp.zeros((tok_rows, D), jnp.bfloat16)
    section_outs = jnp.zeros((micro_count, tok_rows, D), jnp.bfloat16)
    saved_all = None
    for tick in range(tick_count):
        batch_index = tick - section_id
        is_valid = (batch_index >= 0) & (batch_index < micro_count)
        batch_slot = jnp.clip(batch_index, 0, micro_count - 1)
        own_rows = tokens[batch_slot, 0]
        layer_in = jnp.where(section_id == 0, own_rows, received).astype(jnp.float32)
        cosine, sine = rotary(block_order[batch_slot, 0, cycle_place], tok_rows)
        layer_out, saved = forward_layer(layer_in, cosine, sine, params)
        if saved_all is None:
            saved_all = tuple(
                (jnp.zeros((micro_count,) + item.shape, item.dtype) for item in saved)
            )
        saved_all = tuple(
            (
                keep_slot(buffer, batch_slot, item, is_valid)
                for buffer, item in zip(saved_all, saved)
            )
        )
        outgoing = layer_out.astype(jnp.bfloat16)
        section_outs = keep_slot(section_outs, batch_slot, outgoing, is_valid)
        received = shifted(outgoing, "section", 1)
    grad_received = jnp.zeros((tok_rows, D), jnp.bfloat16)
    input_grads = jnp.zeros((micro_count, tok_rows, D), jnp.float32)
    summed = None
    for tick in range(tick_count):
        batch_index = tick - (section_count - 1 - section_id)
        is_valid = (batch_index >= 0) & (batch_index < micro_count)
        batch_slot = jnp.clip(batch_index, 0, micro_count - 1)
        upstream = jnp.where(
            section_id == section_count - 1, cotangent[batch_slot, 0], grad_received
        ).astype(jnp.float32)
        cosine, sine = rotary(block_order[batch_slot, 0, cycle_place], tok_rows)
        saved = tuple(
            (
                lax.dynamic_index_in_dim(buffer, batch_slot, 0, keepdims=False)
                for buffer in saved_all
            )
        )
        grad_layer_in, raw_grads = backward_layer(
            upstream, cosine, sine, params, saved, cycle_place
        )
        weight_grads = tuple(
            (jnp.where(is_valid, grad_term, jnp.zeros_like(grad_term)) for grad_term in raw_grads)
        )
        outgoing = grad_layer_in.astype(jnp.bfloat16)
        kept_grad = jnp.where(section_id == 0, grad_layer_in, outgoing.astype(jnp.float32))
        input_grads = keep_slot(input_grads, batch_slot, kept_grad, is_valid)
        summed = (
            weight_grads
            if summed is None
            else tuple((left + right for left, right in zip(summed, weight_grads)))
        )
        grad_received = shifted(outgoing, "section", -1)
    if use_kernels():
        summed = scatter_grads(summed)
    else:
        raised = [grad_term[None] for grad_term in summed]
        summed = (
            lax.psum_scatter(raised[0], ("ctx", "wshard"), scatter_dimension=1, tiled=True),
            lax.psum_scatter(raised[1], ("ctx", "wshard"), scatter_dimension=1, tiled=True),
            lax.psum_scatter(raised[2], ("ctx", "wshard"), scatter_dimension=1, tiled=True),
            lax.psum_scatter(raised[3], ("ctx", "wshard"), scatter_dimension=1, tiled=True),
            lax.psum_scatter(raised[4], ("ctx", "wshard"), scatter_dimension=1, tiled=True),
            lax.psum_scatter(raised[5], ("ctx", "wshard"), scatter_dimension=1, tiled=True),
        )
    return (
        section_outs[None, :, None],
        input_grads[None, :, None],
        summed[0],
        summed[1],
        summed[2],
        summed[3],
        summed[4],
        summed[5],
    )


def swap_kernel(cycle, in_ref, out_ref, own_sem, send, recv):
    me = lax.axis_index("ctx")
    barrier = pltpu.get_barrier_semaphore()
    peers = [lax.rem(me + d, cycle) for d in range(1, cycle)]
    for peer in peers:
        pl.semaphore_signal(barrier, inc=1, device_id={"ctx": peer}, device_id_type=MESH)
    pl.semaphore_wait(barrier, cycle - 1)
    copies = [
        pltpu.make_async_remote_copy(
            in_ref.at[peer], out_ref.at[me], send.at[index], recv.at[index],
            device_id={"ctx": peer}, device_id_type=MESH)
        for index, peer in enumerate(peers)
    ]
    for copy in copies:
        copy.start()
    own = pltpu.make_async_copy(in_ref.at[me], out_ref.at[me], own_sem)
    own.start()
    own.wait()
    for copy in copies:
        copy.wait()


def swap(pieces, collective):
    cycle = pieces.shape[0]
    return pl.pallas_call(
        lambda *refs: swap_kernel(cycle, *refs),
        out_shape=jax.ShapeDtypeStruct(pieces.shape, pieces.dtype),
        in_specs=[pl.BlockSpec(memory_space=pl.ANY)],
        out_specs=pl.BlockSpec(memory_space=pl.ANY),
        scratch_shapes=[
            pltpu.SemaphoreType.DMA,
            pltpu.SemaphoreType.DMA((cycle - 1,)),
            pltpu.SemaphoreType.DMA((cycle - 1,)),
        ],
        compiler_params=pltpu.CompilerParams(collective_id=collective, has_side_effects=True),
        name="swap_narrow" if collective == 2 else "swap_wide",
    )(pieces)


def dot_last(left, right):
    return lax.dot_general(left, right, (((1,), (1,)), ((), ())), preferred_element_type=jnp.float32)


def dot_first(left, right):
    return lax.dot_general(left, right, (((0,), (0,)), ((), ())), preferred_element_type=jnp.float32)


def attend_kernel(width, block, rows_ref, out_ref):
    start = pl.multiple_of(pl.program_id(0) * block, block)
    for low in range(0, width, HEAD_DIM):
        query = rows_ref[pl.ds(start, block), low : low + HEAD_DIM]
        key = rows_ref[:, width + low : width + low + HEAD_DIM]
        value = rows_ref[:, 2 * width + low : 2 * width + low + HEAD_DIM]
        scores = dot_last(query, key) * HEAD_DIM ** (-0.5)
        exponents = jnp.exp(scores - jnp.max(scores, axis=-1, keepdims=True))
        total = jnp.sum(exponents, axis=-1, keepdims=True)
        weighted = jnp.dot(exponents.astype(jnp.bfloat16), value, preferred_element_type=jnp.float32)
        out_ref[:, low : low + HEAD_DIM] = (weighted / total).astype(jnp.bfloat16)


def attend_rows(rows):
    length, width = rows.shape[0], rows.shape[1] // 3
    block = min(256, length)
    return pl.pallas_call(
        lambda *refs: attend_kernel(width, block, *refs),
        grid=(length // block,),
        out_shape=jax.ShapeDtypeStruct((length, width), jnp.bfloat16),
        in_specs=[pl.BlockSpec(rows.shape, lambda i: (0, 0))],
        out_specs=pl.BlockSpec((block, width), lambda i: (i, 0)),
        compiler_params=pltpu.CompilerParams(vmem_limit_bytes=48 * 1024 * 1024),
        name="attend_rows",
    )(rows)


def attend_back_kernel(width, block, steps, rows_ref, grad_ref, out_ref, key_sum, value_sum):
    step = pl.program_id(0)
    start = pl.multiple_of(step * block, block)

    @pl.when(step == 0)
    def _():
        key_sum[...] = jnp.zeros_like(key_sum)
        value_sum[...] = jnp.zeros_like(value_sum)

    scale = HEAD_DIM ** (-0.5)
    for low in range(0, width, HEAD_DIM):
        high = low + HEAD_DIM
        query = rows_ref[pl.ds(start, block), low:high]
        grad = grad_ref[pl.ds(start, block), low:high]
        key = rows_ref[:, width + low : width + high]
        value = rows_ref[:, 2 * width + low : 2 * width + high]
        scores = dot_last(query, key) * scale
        exponents = jnp.exp(scores - jnp.max(scores, axis=-1, keepdims=True))
        probs = exponents * (1.0 / jnp.sum(exponents, axis=-1, keepdims=True))
        upstream = dot_last(grad, value)
        delta = jnp.sum(probs * upstream, axis=-1, keepdims=True)
        grad_scores = (probs * (upstream - delta)).astype(jnp.bfloat16)
        query_grad = jnp.dot(grad_scores, key, preferred_element_type=jnp.float32) * scale
        out_ref[pl.ds(start, block), low:high] = query_grad.astype(jnp.bfloat16)
        key_sum[:, low:high] += dot_first(grad_scores, query)
        value_sum[:, low:high] += dot_first(probs.astype(jnp.bfloat16), grad)

    @pl.when(step == steps - 1)
    def _():
        out_ref[:, width : 2 * width] = (key_sum[...] * scale).astype(jnp.bfloat16)
        out_ref[:, 2 * width :] = value_sum[...].astype(jnp.bfloat16)


def attend_back(rows, grads):
    length, width = grads.shape
    block = min(256, length)
    steps = length // block
    return pl.pallas_call(
        lambda *refs: attend_back_kernel(width, block, steps, *refs),
        grid=(steps,),
        out_shape=jax.ShapeDtypeStruct(rows.shape, jnp.bfloat16),
        in_specs=[
            pl.BlockSpec(rows.shape, lambda i: (0, 0)),
            pl.BlockSpec(grads.shape, lambda i: (0, 0)),
        ],
        out_specs=pl.BlockSpec(rows.shape, lambda i: (0, 0)),
        scratch_shapes=[pltpu.VMEM(grads.shape, jnp.float32), pltpu.VMEM(grads.shape, jnp.float32)],
        compiler_params=pltpu.CompilerParams(vmem_limit_bytes=48 * 1024 * 1024),
        name="attend_back",
    )(rows, grads)


def to_units(values, micro, cycle):
    groups = cycle // micro
    rows, kinds = values.shape[0] // micro, values.shape[1] // D
    parts = values.reshape(micro, rows, kinds, groups, D // groups)
    return parts.transpose(0, 3, 1, 2, 4).reshape(cycle, rows, kinds * D // groups)


def from_units(pieces, micro):
    cycle, rows, width = pieces.shape
    groups = cycle // micro
    kinds = width * groups // D
    parts = pieces.reshape(micro, groups, rows, kinds, D // groups)
    return parts.transpose(0, 2, 3, 1, 4).reshape(micro * rows, kinds * D)


def to_sequence(values, micro, cycle):
    kinds = values.shape[1] // D
    received = swap(to_units(values, micro, cycle), 2 if kinds == 1 else 3)
    return received.reshape(-1, received.shape[2])


def from_sequence(rows, micro, cycle):
    kinds = 2 if rows.shape[1] * cycle // micro == D else 3
    received = swap(rows.reshape(cycle, -1, rows.shape[1]), kinds)
    return from_units(received, micro)


def halves(values):
    half_width = HEAD_DIM // 2
    first = lax.broadcasted_iota(jnp.int32, values.shape, 1) % HEAD_DIM < half_width
    return (first, jnp.roll(values, -half_width, axis=1), jnp.roll(values, half_width, axis=1))


def turn(values):
    first, ahead, behind = halves(values)
    return jnp.where(first, -ahead, behind)


def turn_back(values):
    first, ahead, behind = halves(values)
    return jnp.where(first, ahead, -behind)


def fast_forward(layer_in, cosine, sine, params, micro, cycle):
    gain_one, w_qkv, w_out, gain_two, w_in, w_down = params
    normed_one, _ = normalize(layer_in)
    mixed = jnp.dot(
        (normed_one * gain_one.astype(jnp.float32)).astype(jnp.bfloat16),
        w_qkv,
        preferred_element_type=jnp.float32,
    )
    rotated = mixed[:, : 2 * D]
    rotated = rotated * cosine + turn(rotated) * sine
    mixed = jnp.concatenate([rotated, mixed[:, 2 * D :]], axis=-1).astype(jnp.bfloat16)
    rows = to_sequence(mixed, micro, cycle)
    attended = from_sequence(attend_rows(rows), micro, cycle)
    hidden = layer_in + jnp.dot(attended, w_out, preferred_element_type=jnp.float32)
    normed_two, _ = normalize(hidden)
    gate_up = jnp.dot(
        (normed_two * gain_two.astype(jnp.float32)).astype(jnp.bfloat16),
        w_in,
        preferred_element_type=jnp.float32,
    )
    product = (jax.nn.gelu(gate_up[:, :FF], approximate=False) * gate_up[:, FF:]).astype(
        jnp.bfloat16
    )
    layer_out = hidden + jnp.dot(product, w_down, preferred_element_type=jnp.float32)
    return (layer_out, (layer_in, hidden, gate_up, rows, attended))


def fast_backward(upstream, cosine, sine, params, saved, micro, cycle):
    gain_one, w_qkv, w_out, gain_two, w_in, w_down = params
    layer_in, hidden, gate_up, rows, attended = saved
    grad_branch = upstream.astype(jnp.bfloat16)
    up_part = gate_up[:, FF:]
    activated, gelu_pull = jax.vjp(
        lambda gate_in: jax.nn.gelu(gate_in, approximate=False), gate_up[:, :FF]
    )
    product = (activated * up_part).astype(jnp.bfloat16)
    grad_down = dot_first(product, grad_branch)
    grad_product = dot_last(grad_branch, w_down)
    grad_gate_up = jnp.concatenate(
        [gelu_pull(grad_product * up_part)[0], grad_product * activated], axis=-1
    ).astype(jnp.bfloat16)
    normed_two, inverse_two = normalize(hidden)
    gain_two_full = gain_two.astype(jnp.float32)
    grad_in = dot_first((normed_two * gain_two_full).astype(jnp.bfloat16), grad_gate_up)
    grad_normed_two = dot_last(grad_gate_up, w_in)
    grad_gain_two = jnp.sum(grad_normed_two * normed_two, axis=0)
    grad_hidden = upstream + norm_back(grad_normed_two * gain_two_full, normed_two, inverse_two)
    grad_attn_out = grad_hidden.astype(jnp.bfloat16)
    grad_out = dot_first(attended, grad_attn_out)
    grad_attended = dot_last(grad_attn_out, w_out).astype(jnp.bfloat16)
    grad_rows = attend_back(rows, to_sequence(grad_attended, micro, cycle))
    grad_raw = from_sequence(grad_rows, micro, cycle)
    rotated = grad_raw[:, : 2 * D].astype(jnp.float32)
    rotated = (rotated * cosine + turn_back(rotated * sine)).astype(jnp.bfloat16)
    grad_mixed = jnp.concatenate([rotated, grad_raw[:, 2 * D :]], axis=-1)
    normed_one, inverse_one = normalize(layer_in)
    gain_one_full = gain_one.astype(jnp.float32)
    grad_qkv = dot_first((normed_one * gain_one_full).astype(jnp.bfloat16), grad_mixed)
    grad_normed_one = dot_last(grad_mixed, w_qkv)
    grad_gain_one = jnp.sum(grad_normed_one * normed_one, axis=0)
    grad_layer_in = grad_hidden + norm_back(
        grad_normed_one * gain_one_full, normed_one, inverse_one
    )
    return (grad_layer_in, (grad_gain_one, grad_qkv, grad_out, grad_gain_two, grad_in, grad_down))


def fast_body(tokens, block_order, cotangent, *weights):
    section_id = lax.axis_index("section")
    section_count = lax.axis_size("section")
    cycle = lax.axis_size("ctx")
    micro, _, tok_rows, _ = tokens.shape
    params = gather_params(*weights)
    blocks = block_order[:, 0, lax.axis_index("ctx")]
    tables = [rotary(blocks[index], tok_rows) for index in range(micro)]
    cosine, sine = (
        jnp.tile(jnp.concatenate([table[kind][:, 0] for table in tables], axis=0), (1, 2 * HEADS))
        for kind in range(2)
    )
    own_rows = tokens[:, 0].reshape(micro * tok_rows, D)
    upstream_rows = cotangent[:, 0].reshape(micro * tok_rows, D)
    layer_in = own_rows
    for tick in range(section_count):
        layer_out, saved = fast_forward(
            layer_in.astype(jnp.float32), cosine, sine, params, micro, cycle
        )
        outgoing = layer_out.astype(jnp.bfloat16)
        if tick < section_count - 1:
            layer_in = jnp.where(section_id == 0, own_rows, shifted(outgoing, "section", 1))
    section_outs = outgoing
    upstream = upstream_rows
    for tick in range(section_count):
        grad_layer_in, summed = fast_backward(
            upstream.astype(jnp.float32), cosine, sine, params, saved, micro, cycle
        )
        outgoing = grad_layer_in.astype(jnp.bfloat16)
        if tick < section_count - 1:
            upstream = jnp.where(
                section_id == section_count - 1, upstream_rows, shifted(outgoing, "section", -1)
            )
    input_grads = jnp.where(section_id == 0, grad_layer_in, outgoing.astype(jnp.float32))
    shape = (1, micro, 1, tok_rows, D)
    return (section_outs.reshape(shape), input_grads.reshape(shape)) + scatter_grads(summed)


def body(tokens, *rest):
    micro, cycle = tokens.shape[0], lax.axis_size("ctx")
    if use_kernels() and cycle % micro == 0 and HEADS % (cycle // micro) == 0:
        return fast_body(tokens, *rest)
    return staged_body(tokens, *rest)


def solution(mesh):
    in_specs = (
        P(None, "wshard", "ctx", None),
        P(None, "wshard", None),
        P(None, "wshard", "ctx", None),
        P("section", ("ctx", "wshard")),
        P("section", ("ctx", "wshard"), None),
        P("section", ("ctx", "wshard"), None),
        P("section", ("ctx", "wshard")),
        P("section", ("ctx", "wshard"), None),
        P("section", ("ctx", "wshard"), None),
    )
    out_specs = (
        P("section", None, "wshard", "ctx", None),
        P("section", None, "wshard", "ctx", None),
        P("section", ("ctx", "wshard")),
        P("section", ("ctx", "wshard"), None),
        P("section", ("ctx", "wshard"), None),
        P("section", ("ctx", "wshard")),
        P("section", ("ctx", "wshard"), None),
        P("section", ("ctx", "wshard"), None),
    )
    return jax.shard_map(body, mesh=mesh, in_specs=in_specs, out_specs=out_specs, check_vma=False)
```
